128 devices in a mesh: ctx: 16 (over z, x_lo, core), tp: 8 (over y, x_hi).
Axes of the slice: x: 4 (x_hi: 2, x_lo: 2; x = x_hi * 2 + x_lo), y: 4, z: 4, core: 2. Of those that a mesh axis runs over, the one named last changes fastest.
Arguments:
- tokens: bfloat16 [64, 256, 2048], P('ctx'), may hold values from -6 to 6
- block_lists: int32 [16, 4], replicated, may hold values from 0 to 15, as said below
- gain_attn: float32 [2048], replicated, may hold values from 0.5 to 1.5
- w_qkv: bfloat16 [2048, 3, 2048], P(None, None, 'tp'), may hold values from -3 to 3
- w_out: bfloat16 [2048, 2048], P('tp'), may hold values from -0.1875 to 0.1875
- gain_mlp: float32 [2048], replicated, may hold values from 0.5 to 1.5
- w_up: bfloat16 [2048, 8192], P(None, 'tp'), may hold values from -0.125 to 0.125
- w_down: bfloat16 [8192, 2048], P('tp'), may hold values from -0.09375 to 0.09375
Outputs:
- layer_out: bfloat16 [64, 256, 2048], P('ctx', None, 'tp')
The draws below stay inside these ranges and needn't reach their ends.
Inputs may be any that keep to these rules, and one draw needn't show every extreme that they name: `block_lists`: row i starts with i itself, then i - 1 (0 for row 0); the remaining entries step back from i by a stride of 2 to 4 blocks drawn for each row, one and two strides, clamped at 0; every entry lies between 0 and i.
All inputs are finite; a program needn't handle non-finite values.
Results may differ from the reference program's by a relative error of at most 0.015.
Values may be sent and summed in bfloat16 or wider, within the bound.
A program may use at most 128 MiB of HBM per device.

```python
import jax
import jax.numpy as jnp
from jax import lax

D = 2048
H = 16
HD = 128
FF = 8192
COLS = 256
ROWS_DEV = 4
NL = 4
N_CTX = 16
N_TP = 8


def draw_tokens(key, part):
    key = jax.random.fold_in(key, 11)
    key_one = jax.random.fold_in(key, 0)
    shape = (ROWS_DEV * N_CTX, COLS, D)
    base = jax.random.normal(key_one, shape, jnp.float32)
    return jnp.clip(base, -6.0, 6.0).astype(jnp.bfloat16)


def draw_block_lists(key, part):
    key = jax.random.fold_in(key, 37)
    block_ids = jnp.arange(N_CTX, dtype=jnp.int32)[:, None]
    strides = jax.random.randint(key, (N_CTX, 1), 2, 5, dtype=jnp.int32)
    entries = jnp.arange(NL, dtype=jnp.int32)[None, :]
    back = jnp.where(entries == 0, 0, jnp.where(entries == 1, 1, (entries - 1) * strides))
    return jnp.maximum(block_ids - back, 0).astype(jnp.int32)


def draw_w_qkv(key, part):
    key = jax.random.fold_in(key, 23)
    key_one = jax.random.fold_in(key, 0)
    weights = jax.random.normal(key_one, (D, 3, H * HD), jnp.float32) * D ** (-0.5)
    return jnp.clip(weights, -3.0, 3.0).astype(jnp.bfloat16)


def with_spikes(values, key, source, target, shards_of, factor):
    owner, partner = [(jnp.arange(values.shape[dim]) // (values.shape[dim] // shards_of)).reshape([-1 if axis == dim else 1 for axis in range(values.ndim)]) for dim in (source, target)]
    chosen = jax.random.permutation(key, shards_of)[partner]
    strong = (owner == chosen) | (owner == (partner + shards_of // 2) % shards_of)
    return jnp.where(strong, factor * values, values)


def levels(stream_key, dims, cuts, smallest, high):
    factor_of = 1.0
    for dim, blocks in cuts:
        draws = jax.random.uniform(jax.random.fold_in(jax.random.fold_in(stream_key, 6), dim), (blocks,), jnp.float32, smallest / len(cuts), high / len(cuts))
        factor_of = factor_of * jnp.repeat(jnp.exp(draws), dims[dim] // blocks).reshape((-1,) + (1,) * (len(dims) - 1 - dim))
    return factor_of


def noise(own_key, extent, scale, reach, cuts=(), kind=jnp.bfloat16):
    level = levels(own_key, extent, cuts, -0.22, 0.18) if cuts else 1.0
    array = jax.random.normal(own_key, extent, jnp.float32) * scale * level
    return jnp.minimum(jnp.maximum(array, -reach), reach).astype(kind)


def gaussian_with(own_key, dims, deviation, most, cuts, heavy, kind=jnp.bfloat16):
    values = deviation * jax.random.normal(own_key, dims, jnp.float32)
    if cuts:
        values = values * levels(own_key, dims, cuts, -0.22, 0.18)
    return jnp.clip(with_spikes(values, jax.random.fold_in(own_key, 3), *heavy), -most, most).astype(kind)


def setup_inputs(seed: int = 0) -> dict:
    key_list = jax.random.split(jax.random.key(seed), 9)
    tokens = draw_tokens(jax.random.fold_in(key_list[8], 71), 0)
    block_lists = draw_block_lists(jax.random.fold_in(key_list[8], 71), 0)
    gain_attn = jnp.clip(1.0 + 0.1 * jax.random.normal(key_list[2], (D,), jnp.float32), 0.5, 1.5)
    w_qkv = draw_w_qkv(jax.random.fold_in(key_list[8], 71), 0)
    w_out = gaussian_with(key_list[4], (H * HD, D), (H * HD) ** -0.5, 0.1875, ((0, 8),), (0, 1, 8, 2.0))
    gain_mlp = jnp.clip(1.0 + 0.1 * jax.random.normal(key_list[5], (D,), jnp.float32), 0.5, 1.5)
    w_up = noise(key_list[6], (D, FF), D ** -0.5, 0.125, ((1, 8),))
    w_down = gaussian_with(key_list[7], (FF, D), FF ** -0.5, 0.09375, ((0, 8),), (0, 1, 8, 2.0))
    return dict(tokens=tokens, block_lists=block_lists, gain_attn=gain_attn, w_qkv=w_qkv, w_out=w_out, gain_mlp=gain_mlp, w_up=w_up, w_down=w_down)


negative_fill = -1e+30

def layer_norm(values, gain):
    centre = lax.optimization_barrier(jnp.mean(values, axis=-1, keepdims=True))
    centred = values - centre
    variance = lax.optimization_barrier(jnp.mean(centred * centred, axis=-1, keepdims=True))
    return centred * lax.rsqrt(variance + 1e-05) * gain

def reference(tokens, block_lists, gain_attn, w_qkv, w_out, gain_mlp, w_up, w_down):
    slab_rows = tokens.shape[0]
    slab_cols = tokens.shape[1]
    flat_tokens = tokens.reshape(slab_rows * slab_cols, D).astype(jnp.float32)
    normed = layer_norm(flat_tokens, gain_attn).astype(jnp.bfloat16)
    projected = jnp.dot(normed, w_qkv.reshape(D, 3 * H * HD), preferred_element_type=jnp.float32)
    projected = projected.astype(jnp.bfloat16).reshape(slab_rows, slab_cols, 3, H, HD)
    stacked = jnp.transpose(projected.astype(jnp.float32), (2, 3, 0, 1, 4))
    row_ids = jnp.arange(slab_rows)
    row_blocks = row_ids // ROWS_DEV
    listed = jnp.any(block_lists[:, :, None] == jnp.arange(N_CTX)[None, None, :], axis=1)
    column_allowed = listed[row_blocks][:, row_blocks] & (row_ids[None, :] < row_ids[:, None])
    col_ids = jnp.arange(slab_cols)
    row_allowed = col_ids[None, :] <= col_ids[:, None]
    score_scale = HD ** (-0.5)

    def one_head(head_inputs):
        queries, key_heads, value_heads = head_inputs
        row_scores = jnp.einsum('rcd,red->rce', queries, key_heads, precision=lax.Precision.HIGHEST) * score_scale
        col_scores = jnp.einsum('rcd,scd->rcs', queries, key_heads, precision=lax.Precision.HIGHEST) * score_scale
        row_mask = row_allowed[None, :, :]
        col_mask = column_allowed[:, None, :]
        row_scores = jnp.where(row_mask, row_scores, negative_fill)
        col_scores = jnp.where(col_mask, col_scores, negative_fill)
        largest = jnp.maximum(lax.optimization_barrier(jnp.max(row_scores, axis=-1)), lax.optimization_barrier(jnp.max(col_scores, axis=-1)))
        row_weights = jnp.where(row_mask, jnp.exp(row_scores - largest[..., None]), 0.0)
        col_weights = jnp.where(col_mask, jnp.exp(col_scores - largest[..., None]), 0.0)
        weight_sum = lax.optimization_barrier(jnp.sum(row_weights, axis=-1)) + lax.optimization_barrier(jnp.sum(col_weights, axis=-1))
        weighted = jnp.einsum('rce,red->rcd', row_weights, value_heads, precision=lax.Precision.HIGHEST)
        weighted = weighted + jnp.einsum('rcs,scd->rcd', col_weights, value_heads, precision=lax.Precision.HIGHEST)
        return weighted / weight_sum[..., None]
    head_outputs = lax.map(one_head, (stacked[0], stacked[1], stacked[2]))
    attended = jnp.transpose(head_outputs, (1, 2, 0, 3)).astype(jnp.bfloat16).reshape(slab_rows * slab_cols, H * HD)
    heads_here = H // N_TP
    head_total = jnp.zeros((slab_rows * slab_cols, D), jnp.float32)
    for group_index in range(N_TP):
        low = group_index * heads_here * HD
        high = low + heads_here * HD
        term = jnp.dot(attended[:, low:high], w_out[low:high], preferred_element_type=jnp.float32)
        term = lax.optimization_barrier(term.astype(jnp.bfloat16))
        head_total = head_total + term.astype(jnp.float32)
    residual = flat_tokens + head_total
    normed_mlp = layer_norm(residual, gain_mlp).astype(jnp.bfloat16)
    units_here = FF // N_TP
    mlp_total = jnp.zeros((slab_rows * slab_cols, D), jnp.float32)
    for group_index in range(N_TP):
        low = group_index * units_here
        high = low + units_here
        upward = jnp.dot(normed_mlp, w_up[:, low:high], preferred_element_type=jnp.float32)
        activated = jax.nn.gelu(upward).astype(jnp.bfloat16)
        term = jnp.dot(activated, w_down[low:high], preferred_element_type=jnp.float32)
        term = lax.optimization_barrier(term.astype(jnp.bfloat16))
        mlp_total = mlp_total + term.astype(jnp.float32)
    return (residual + mlp_total).astype(jnp.bfloat16).reshape(slab_rows, slab_cols, D)
```

```python
import functools

import jax
import jax.numpy as jnp
from jax import lax
from jax.experimental import pallas as pl
from jax.experimental.pallas import tpu as pltpu
from jax.sharding import PartitionSpec as P

HD = 128
MESH = pl.DeviceIdType.MESH
NEG = -1e30
BF = jnp.bfloat16
F32 = jnp.float32


def remote(src, dst, send_sem, recv_sem, device):
    return pltpu.make_async_remote_copy(
        src_ref=src, dst_ref=dst, send_sem=send_sem, recv_sem=recv_sem, device_id=device, device_id_type=MESH
    )


def layer_norm(values, gain):
    centre = jnp.mean(values, axis=-1, keepdims=True)
    centred = values - centre
    variance = jnp.mean(centred * centred, axis=-1, keepdims=True)
    return centred * lax.rsqrt(variance + 1e-05) * gain


def dot(a, b):
    return jnp.dot(a, b, preferred_element_type=F32)


def dot_t(a, b):
    return lax.dot_general(a, b, (((1,), (1,)), ((), ())), preferred_element_type=F32)


def attn_kernel(
    lists, tok_ref, gain_ref, wqkv_ref, wout_ref, att_ref, wfull_ref,
    tok, wqkv, normed, qkv, recv, colout, ret, acc, maxes, sums,
    load_sem, own_sem, send_sem, recv_sem, back_send, back_recv, wo_send, wo_recv, wc_send, wc_recv,
):
    n_ctx, rows, cols, feats = 16, 4, 256, 768
    share = cols // n_ctx
    ctx = lax.axis_index("ctx")
    tp = lax.axis_index("tp")
    core = lax.rem(ctx, 2)
    sibling = ctx + 1 - 2 * core

    loads = [pltpu.make_async_copy(wqkv_ref, wqkv, load_sem.at[4])]
    for r in range(rows):
        loads.append(pltpu.make_async_copy(tok_ref.at[pl.ds(r * cols, cols), :], tok.at[r], load_sem.at[r]))
    loads[1].start()
    loads[0].start()
    for r in range(1, rows):
        loads[r + 1].start()
    own_w = pltpu.make_async_copy(wout_ref, wfull_ref.at[pl.ds(pl.multiple_of(tp * 256, 256), 256), :], own_sem.at[0])
    own_w.start()

    barrier = pltpu.get_barrier_semaphore()
    for k in range(1, n_ctx):
        pl.semaphore_signal(barrier, inc=1, device_id={"ctx": lax.rem(ctx + k, n_ctx)}, device_id_type=MESH)
    for k in range(1, 8):
        pl.semaphore_signal(barrier, inc=1, device_id={"tp": lax.rem(tp + k, 8)}, device_id_type=MESH)
    pl.semaphore_wait(barrier, n_ctx - 1 + 7)

    def half(owner, which):
        return pl.ds(pl.multiple_of(owner * 256 + which * 128, 128), 128)

    gather = []
    for k in range(1, 8):
        gather.append(
            remote(
                wout_ref.at[pl.ds(pl.multiple_of(core * 128, 128), 128), :],
                wfull_ref.at[half(tp, core), :],
                wo_send.at[k - 1], wo_recv.at[k - 1], {"tp": lax.rem(tp + k, 8)},
            )
        )
        gather[-1].start()

    loads[0].wait()

    def row_share(j):
        return pl.ds(pl.multiple_of(j * share, share), share)

    @pl.loop(0, rows)
    def _(r):
        pltpu.make_async_copy(tok_ref.at[pl.ds(0, cols), :], tok.at[r], load_sem.at[r]).wait()

        @pl.loop(0, cols // 64)
        def _(b):
            part = pl.ds(pl.multiple_of(b * 64, 64), 64)
            normed[part, :] = layer_norm(tok[r, part, :].astype(F32), gain_ref[...]).astype(BF)

        for n in range(3):
            qkv[r, :, n * 256 : (n + 1) * 256] = dot(normed[...], wqkv[:, n * 256 : (n + 1) * 256]).astype(BF)
        for k in range(1, n_ctx):
            j = lax.rem(ctx + k, n_ctx)
            remote(
                qkv.at[r, row_share(j), :], recv.at[ctx, r], send_sem.at[k - 1], recv_sem.at[k - 1], {"ctx": j}
            ).start()

    own_block = pltpu.make_async_copy(qkv.at[:, row_share(ctx), :], recv.at[ctx], own_sem.at[1])
    own_block.start()

    causal = lax.broadcasted_iota(jnp.int32, (cols, cols), 1) <= lax.broadcasted_iota(jnp.int32, (cols, cols), 0)

    @pl.loop(0, rows)
    def _(r):
        for h in range(2):
            q = qkv[r, :, h * HD : (h + 1) * HD]
            key = qkv[r, :, 256 + h * HD : 256 + (h + 1) * HD]
            val = qkv[r, :, 512 + h * HD : 512 + (h + 1) * HD]
            scores = jnp.where(causal, dot_t(q, key) * HD ** (-0.5), NEG)
            top = jnp.max(scores, axis=-1, keepdims=True)
            weights = jnp.where(causal, jnp.exp(scores - top), 0.0)
            acc[r, :, h * HD : (h + 1) * HD] = dot(weights.astype(BF), val)
            maxes[r, :, h * HD : (h + 1) * HD] = jnp.broadcast_to(top, (cols, HD))
            sums[r, :, h * HD : (h + 1) * HD] = jnp.broadcast_to(jnp.sum(weights, axis=-1, keepdims=True), (cols, HD))

    own_block.wait()
    for k in range(1, n_ctx):
        source = lax.rem(ctx + n_ctx - k, n_ctx)
        remote(
            recv.at[source], recv.at[source], send_sem.at[k - 1], recv_sem.at[k - 1], {"ctx": source}
        ).wait_recv()

    q_id = lax.broadcasted_iota(jnp.int32, (64, 256), 0)
    k_id = lax.broadcasted_iota(jnp.int32, (64, 256), 1)
    entry = k_id // 64
    same = lax.rem(q_id, 16) == lax.rem(k_id, 16)
    earlier = same & (entry == 0) & (lax.rem(k_id, 64) // 16 < q_id // 16)
    lane = lax.broadcasted_iota(jnp.int32, (64, HD), 1)

    @pl.loop(0, n_ctx)
    def _(i):
        ids = [lists[i, l] for l in range(4)]
        fresh = []
        for l in range(1, 4):
            new = jnp.int32(1)
            for before in range(l):
                new = new * (ids[l] != ids[before]).astype(jnp.int32)
            fresh.append(new)
        usable = jnp.where(entry == 1, fresh[0], jnp.where(entry == 2, fresh[1], fresh[2]))
        mask = earlier | (same & (entry > 0) & (usable > 0))
        stats = jnp.zeros((64, HD), F32)
        for h in range(2):
            q = recv[i, :, :, h * HD : (h + 1) * HD].reshape(64, HD)
            key = jnp.concatenate(
                [recv[b, :, :, 256 + h * HD : 256 + (h + 1) * HD].reshape(64, HD) for b in ids], axis=0
            )
            val = jnp.concatenate(
                [recv[b, :, :, 512 + h * HD : 512 + (h + 1) * HD].reshape(64, HD) for b in ids], axis=0
            )
            scores = jnp.where(mask, dot_t(q, key) * HD ** (-0.5), NEG)
            top = jnp.max(scores, axis=-1, keepdims=True)
            weights = jnp.where(mask, jnp.exp(scores - top), 0.0)
            total = jnp.sum(weights, axis=-1, keepdims=True)
            part = dot(weights.astype(BF), val) / jnp.maximum(total, 1.0)
            colout[i, :, :, h * HD : (h + 1) * HD] = part.astype(BF).reshape(4, 16, HD)
            top_hi = top.astype(BF).astype(F32)
            top_mid = (top - top_hi).astype(BF).astype(F32)
            top_lo = top - top_hi - top_mid
            total_hi = total.astype(BF).astype(F32)
            pieces = [top_hi, top_mid, top_lo, total_hi, total - total_hi]
            for n, piece in enumerate(pieces):
                stats = jnp.where(lane == 8 * h + n, piece, stats)
        colout[i, :, :, 256:384] = stats.astype(BF).reshape(4, 16, HD)

    own_back = pltpu.make_async_copy(colout.at[ctx], ret.at[ctx], own_sem.at[1])
    own_back.start()
    for k in range(1, n_ctx):
        j = lax.rem(ctx + k, n_ctx)
        remote(colout.at[j], ret.at[ctx], back_send.at[k - 1], back_recv.at[k - 1], {"ctx": j}).start()

    forwards = []
    for k in range(1, 8):
        source = lax.rem(tp + 8 - k, 8)
        gather[k - 1].wait_recv()
        place = wfull_ref.at[half(source, core), :]
        forwards.append(remote(place, place, wc_send.at[k - 1], wc_recv.at[k - 1], {"ctx": sibling}))
        forwards[-1].start()

    own_back.wait()
    for k in range(1, n_ctx):
        source = lax.rem(ctx + n_ctx - k, n_ctx)
        remote(
            ret.at[source], ret.at[source], back_send.at[k - 1], back_recv.at[k - 1], {"ctx": source}
        ).wait_recv()

    @pl.loop(0, rows)
    def _(r):
        stats = ret[:, r, :, 256:384].reshape(cols, HD).astype(F32)
        for h in range(2):
            lanes = slice(h * HD, (h + 1) * HD)
            col_top = stats[:, 8 * h : 8 * h + 1] + stats[:, 8 * h + 1 : 8 * h + 2] + stats[:, 8 * h + 2 : 8 * h + 3]
            col_sum = stats[:, 8 * h + 3 : 8 * h + 4] + stats[:, 8 * h + 4 : 8 * h + 5]
            row_top = maxes[r, :, lanes]
            top = jnp.maximum(row_top, col_top)
            row_scale = jnp.exp(row_top - top)
            col_scale = jnp.exp(col_top - top) * col_sum
            part = ret[:, r, :, lanes].reshape(cols, HD).astype(F32)
            merged = (acc[r, :, lanes] * row_scale + part * col_scale) / (sums[r, :, lanes] * row_scale + col_scale)
            att_ref[pl.ds(pl.multiple_of(r * cols, cols), cols), lanes] = merged.astype(BF)

    for k in range(1, n_ctx):
        source = lax.rem(ctx + n_ctx - k, n_ctx)
        remote(
            recv.at[source], recv.at[source], send_sem.at[k - 1], recv_sem.at[k - 1], {"ctx": source}
        ).wait_send()
        remote(
            ret.at[source], ret.at[source], back_send.at[k - 1], back_recv.at[k - 1], {"ctx": source}
        ).wait_send()
    for k in range(7):
        gather[k].wait_send()
        forwards[k].wait()
    own_w.wait()


def mlp_kernel(
    att_ref, tok_ref, wout_ref, gain_ref, wup_ref, wdown_ref, out_ref,
    att, tok, wo, wu, wd, res, normed, act, terms, share, came,
    load_sem, ag_send, ag_recv, rs_send, rs_recv,
):
    chunks, chunk = 4, 256
    tp = lax.axis_index("tp")

    barrier = pltpu.get_barrier_semaphore()
    for k in range(1, 8):
        pl.semaphore_signal(barrier, inc=1, device_id={"tp": lax.rem(tp + k, 8)}, device_id_type=MESH)
    pl.semaphore_wait(barrier, 7)

    def feats(d):
        return pl.ds(pl.multiple_of(d * 256, 256), 256)

    def rows_of(c):
        return pl.ds(pl.multiple_of(c * chunk, chunk), chunk)

    def gather(c, k):
        return remote(
            att_ref.at[rows_of(c), :], att.at[rows_of(c), feats(tp)],
            ag_send.at[c, k - 1], ag_recv.at[c, k - 1], {"tp": lax.rem(tp + k, 8)},
        )

    def scatter(c, k):
        d = lax.rem(tp + k, 8)
        return remote(
            terms.at[rows_of(c), feats(d)], came.at[k - 1, rows_of(c), :],
            rs_send.at[c, k - 1], rs_recv.at[c, k - 1], {"tp": d},
        )

    @pl.loop(0, chunks)
    def _(c):
        for k in range(1, 8):
            gather(c, k).start()

    loads = [
        pltpu.make_async_copy(att_ref, att.at[:, feats(tp)], load_sem.at[0]),
        pltpu.make_async_copy(wout_ref, wo, load_sem.at[1]),
        pltpu.make_async_copy(tok_ref, tok, load_sem.at[2]),
        pltpu.make_async_copy(wup_ref, wu, load_sem.at[3]),
        pltpu.make_async_copy(wdown_ref, wd, load_sem.at[4]),
    ]
    for load in loads:
        load.start()
    for load in loads:
        load.wait()

    @pl.loop(0, chunks)
    def _(c):
        rows = rows_of(c)
        for k in range(1, 8):
            gather(c, k).wait_recv()

        @pl.loop(0, 8)
        def _(n):
            res[:, feats(n)] = tok[rows, feats(n)].astype(F32) + dot(att[rows, :], wo[:, feats(n)])

        @pl.loop(0, chunk // 64)
        def _(b):
            part = pl.ds(pl.multiple_of(b * 64, 64), 64)
            normed[part, :] = layer_norm(res[part, :], gain_ref[...]).astype(BF)

        share[rows, :] = res[:, feats(tp)]

        @pl.loop(0, 4)
        def _(n):
            act[:, feats(n)] = jax.nn.gelu(dot(normed[...], wu[:, feats(n)])).astype(BF)

        for k in range(1, 9):
            d = lax.rem(tp + k, 8)
            terms[rows, feats(d)] = dot(act[...], wd[:, feats(d)]).astype(BF)
            if k < 8:
                scatter(c, k).start()

    @pl.loop(0, chunks)
    def _(c):
        rows = rows_of(c)
        total = share[rows, :] + terms[rows, feats(tp)].astype(F32)
        for k in range(1, 8):
            scatter(c, k).wait_recv()
            total = total + came[k - 1, rows, :].astype(F32)
        out_ref[rows, :] = total.astype(BF)

    @pl.loop(0, chunks)
    def _(c):
        for k in range(1, 8):
            gather(c, k).wait_send()
            scatter(c, k).wait_send()


ANY = pl.BlockSpec(memory_space=pl.ANY)
VMEM = pl.BlockSpec(memory_space=pltpu.VMEM)
SMEM = pl.BlockSpec(memory_space=pltpu.SMEM)
DMA = pltpu.SemaphoreType.DMA


def on_device(tokens, block_lists, gain_attn, w_qkv, w_out, gain_mlp, w_up, w_down):
    rows, cols, width = tokens.shape
    flat = tokens.reshape(rows * cols, width)
    attended, w_full = pl.pallas_call(
        attn_kernel,
        out_shape=(
            jax.ShapeDtypeStruct((rows * cols, 256), BF),
            jax.ShapeDtypeStruct((width, width), BF),
        ),
        in_specs=[SMEM, ANY, VMEM, ANY, ANY],
        out_specs=(VMEM, ANY),
        scratch_shapes=[
            pltpu.VMEM((4, 256, 2048), BF),
            pltpu.VMEM((2048, 768), BF),
            pltpu.VMEM((256, 2048), BF),
            pltpu.VMEM((4, 256, 768), BF),
            pltpu.VMEM((16, 4, 16, 768), BF),
            pltpu.VMEM((16, 4, 16, 384), BF),
            pltpu.VMEM((16, 4, 16, 384), BF),
            pltpu.VMEM((4, 256, 256), F32),
            pltpu.VMEM((4, 256, 256), F32),
            pltpu.VMEM((4, 256, 256), F32),
            DMA((5,)), DMA((2,)), DMA((15,)), DMA((15,)), DMA((15,)), DMA((15,)),
            DMA((7,)), DMA((7,)), DMA((7,)), DMA((7,)),
        ],
        compiler_params=pltpu.CompilerParams(collective_id=0, has_side_effects=True, vmem_limit_bytes=56 << 20),
        name="attn",
    )(block_lists, flat, gain_attn.reshape(1, width), w_qkv.reshape(width, 768), w_out)
    out = pl.pallas_call(
        mlp_kernel,
        out_shape=jax.ShapeDtypeStruct((rows * cols, 256), BF),
        in_specs=[ANY, ANY, ANY, VMEM, ANY, ANY],
        out_specs=VMEM,
        scratch_shapes=[
            pltpu.VMEM((1024, 2048), BF),
            pltpu.VMEM((1024, 2048), BF),
            pltpu.VMEM((2048, 2048), BF),
            pltpu.VMEM((2048, 1024), BF),
            pltpu.VMEM((1024, 2048), BF),
            pltpu.VMEM((256, 2048), F32),
            pltpu.VMEM((256, 2048), BF),
            pltpu.VMEM((256, 1024), BF),
            pltpu.VMEM((1024, 2048), BF),
            pltpu.VMEM((1024, 256), F32),
            pltpu.VMEM((7, 1024, 256), BF),
            DMA((5,)), DMA((4, 7)), DMA((4, 7)), DMA((4, 7)), DMA((4, 7)),
        ],
        compiler_params=pltpu.CompilerParams(collective_id=1, has_side_effects=True, vmem_limit_bytes=56 << 20),
        name="mlp",
    )(attended, flat, w_full, gain_mlp.reshape(1, width), w_up, w_down)
    return out.reshape(rows, cols, 256)


def solution(mesh):
    return jax.shard_map(
        on_device,
        mesh=mesh,
        in_specs=(
            P("ctx", None, None),
            P(),
            P(),
            P(None, None, "tp"),
            P("tp", None),
            P(),
            P(None, "tp"),
            P("tp", None),
        ),
        out_specs=P("ctx", None, "tp"),
        check_vma=False,
    )
```

```python
import functools

import jax
import jax.numpy as jnp
from jax import lax
from jax.experimental import pallas as pl
from jax.experimental.pallas import tpu as pltpu
from jax.sharding import PartitionSpec as P

HD = 128
MESH = pl.DeviceIdType.MESH
NEG = -1e30
CHUNKS = 4
AHEAD = 3
BF = jnp.bfloat16
F32 = jnp.float32


def remote(src, dst, send_sem, recv_sem, device):
    return pltpu.make_async_remote_copy(
        src_ref=src, dst_ref=dst, send_sem=send_sem, recv_sem=recv_sem, device_id=device, device_id_type=MESH
    )


def layer_norm(values, gain):
    centre = jnp.mean(values, axis=-1, keepdims=True)
    centred = values - centre
    variance = jnp.mean(centred * centred, axis=-1, keepdims=True)
    return centred * lax.rsqrt(variance + 1e-05) * gain


def dot(a, b):
    return jnp.dot(a, b, preferred_element_type=F32)


def dot_t(a, b):
    return lax.dot_general(a, b, (((1,), (1,)), ((), ())), preferred_element_type=F32)


class places:
    def __init__(self, tp):
        def other(d):
            return d + 1 - 2 * lax.rem(d, 2)

        self.x = other(tp)
        self.up, self.down, self.far = (lax.rem(tp + step, 8) for step in (2, 6, 4))
        self.up_x, self.down_x, self.far_x = other(self.up), other(self.down), other(self.far)


def attn_kernel(
    lists, tok_ref, gain_ref, wqkv_ref, wout_ref, att_ref, wfull_ref,
    tok, wqkv, normed, qkv, recv, colout, ret, acc, maxes, sums,
    load_sem, own_sem, send_sem, recv_sem, back_send, back_recv, wo_send, wo_recv, wc_send, wc_recv,
):
    n_ctx, rows, cols, feats = 16, 4, 256, 768
    share = cols // n_ctx
    ctx = lax.axis_index("ctx")
    tp = lax.axis_index("tp")
    core = lax.rem(ctx, 2)
    sibling = ctx + 1 - 2 * core

    loads = [pltpu.make_async_copy(wqkv_ref, wqkv, load_sem.at[4])]
    for r in range(rows):
        loads.append(pltpu.make_async_copy(tok_ref.at[pl.ds(r * cols, cols), :], tok.at[r], load_sem.at[r]))
    loads[1].start()
    loads[0].start()
    for r in range(1, rows):
        loads[r + 1].start()
    own_w = pltpu.make_async_copy(wout_ref, wfull_ref.at[pl.ds(pl.multiple_of(tp * 256, 256), 256), :], own_sem.at[0])
    own_w.start()

    barrier = pltpu.get_barrier_semaphore()
    for k in range(1, n_ctx):
        pl.semaphore_signal(barrier, inc=1, device_id={"ctx": lax.rem(ctx + k, n_ctx)}, device_id_type=MESH)
    for k in range(1, 8):
        pl.semaphore_signal(barrier, inc=1, device_id={"tp": lax.rem(tp + k, 8)}, device_id_type=MESH)
    pl.semaphore_wait(barrier, n_ctx - 1 + 7)

    here = places(tp)

    def w_rows(owner, begin=0, size=128):
        return wfull_ref.at[pl.ds(pl.multiple_of(owner * 256 + core * 128 + begin, 64), size), :]

    def pass_on(kind, owner, device, begin=0, size=128):
        place = w_rows(owner, begin, size)
        return remote(place, place, wo_send.at[kind], wo_recv.at[kind], {"tp": device})

    own_half = wout_ref.at[pl.ds(pl.multiple_of(core * 128, 128), 128), :]
    w_first = [
        remote(own_half, w_rows(tp), wo_send.at[kind], wo_recv.at[kind], {"tp": device})
        for kind, device in enumerate((here.x, here.up, here.down))
    ]
    w_across = [pass_on(3, here.x, here.up), pass_on(4, here.x, here.down)]
    w_halves = [pass_on(5, here.down, here.up, 0, 64), pass_on(6, here.up, here.down, 64, 64)]
    w_last = [pass_on(7, here.down_x, here.up, 0, 64), pass_on(8, here.up_x, here.down, 64, 64)]

    def to_sibling(kind, owner):
        place = w_rows(owner)
        return remote(place, place, wc_send.at[kind], wc_recv.at[kind], {"ctx": sibling})

    siblings = [
        to_sibling(kind, owner)
        for kind, owner in enumerate((here.x, here.up, here.down, here.up_x, here.down_x, here.far, here.far_x))
    ]
    for copy in w_first:
        copy.start()

    loads[0].wait()

    def row_share(j):
        return pl.ds(pl.multiple_of(j * share, share), share)

    @pl.loop(0, rows)
    def _(r):
        pltpu.make_async_copy(tok_ref.at[pl.ds(0, cols), :], tok.at[r], load_sem.at[r]).wait()

        for b in range(cols // 64):
            part = slice(b * 64, (b + 1) * 64)
            normed[part, :] = layer_norm(tok[r, part, :].astype(F32), gain_ref[...]).astype(BF)
        for n in range(3):
            qkv[r, :, n * 256 : (n + 1) * 256] = dot(normed[...], wqkv[n]).astype(BF)
        for k in range(1, n_ctx):
            j = lax.rem(ctx + k, n_ctx)
            remote(
                qkv.at[r, row_share(j), :], recv.at[ctx, r], send_sem.at[k - 1], recv_sem.at[k - 1], {"ctx": j}
            ).start()

    own_block = pltpu.make_async_copy(qkv.at[:, row_share(ctx), :], recv.at[ctx], own_sem.at[1])
    own_block.start()

    causal = lax.broadcasted_iota(jnp.int32, (cols, cols), 1) <= lax.broadcasted_iota(jnp.int32, (cols, cols), 0)

    @pl.loop(0, rows)
    def _(r):
        for h in range(2):
            q = qkv[r, :, h * HD : (h + 1) * HD]
            key = qkv[r, :, 256 + h * HD : 256 + (h + 1) * HD]
            val = qkv[r, :, 512 + h * HD : 512 + (h + 1) * HD]
            scores = jnp.where(causal, dot_t(q, key) * HD ** (-0.5), NEG)
            top = jnp.max(scores, axis=-1, keepdims=True)
            weights = jnp.where(causal, jnp.exp(scores - top), 0.0)
            acc[r, :, h * HD : (h + 1) * HD] = dot(weights.astype(BF), val)
            maxes[r, :, h * HD : (h + 1) * HD] = jnp.broadcast_to(top, (cols, HD))
            sums[r, :, h * HD : (h + 1) * HD] = jnp.broadcast_to(jnp.sum(weights, axis=-1, keepdims=True), (cols, HD))

    for copy in w_first:
        copy.wait_recv()
    for copy in w_across + w_halves + siblings[:3]:
        copy.start()

    own_block.wait()
    for k in range(1, n_ctx):
        source = lax.rem(ctx + n_ctx - k, n_ctx)
        remote(
            recv.at[source], recv.at[source], send_sem.at[k - 1], recv_sem.at[k - 1], {"ctx": source}
        ).wait_recv()

    q_id = lax.broadcasted_iota(jnp.int32, (64, 256), 0)
    k_id = lax.broadcasted_iota(jnp.int32, (64, 256), 1)
    entry = k_id // 64
    same = lax.rem(q_id, 16) == lax.rem(k_id, 16)
    earlier = same & (entry == 0) & (lax.rem(k_id, 64) // 16 < q_id // 16)
    lane = lax.broadcasted_iota(jnp.int32, (64, HD), 1)

    def column_block(i):
        ids = [lists[l, i] for l in range(4)]
        fresh = []
        for l in range(1, 4):
            new = jnp.int32(1)
            for before in range(l):
                new = new * (ids[l] != ids[before]).astype(jnp.int32)
            fresh.append(new)
        usable = jnp.where(entry == 1, fresh[0], jnp.where(entry == 2, fresh[1], fresh[2]))
        mask = earlier | (same & (entry > 0) & (usable > 0))
        stats = jnp.zeros((64, HD), F32)
        for h in range(2):
            q = recv[i, :, :, h * HD : (h + 1) * HD].reshape(64, HD)
            key = jnp.concatenate(
                [recv[b, :, :, 256 + h * HD : 256 + (h + 1) * HD].reshape(64, HD) for b in ids], axis=0
            )
            val = jnp.concatenate(
                [recv[b, :, :, 512 + h * HD : 512 + (h + 1) * HD].reshape(64, HD) for b in ids], axis=0
            )
            scores = jnp.where(mask, dot_t(q, key) * HD ** (-0.5), NEG)
            top = jnp.max(scores, axis=-1, keepdims=True)
            weights = jnp.where(mask, jnp.exp(scores - top), 0.0)
            total = jnp.sum(weights, axis=-1, keepdims=True)
            part = dot(weights.astype(BF), val) / jnp.maximum(total, 1.0)
            colout[i, :, :, h * HD : (h + 1) * HD] = part.astype(BF).reshape(4, 16, HD)
            top_hi = top.astype(BF).astype(F32)
            top_mid = (top - top_hi).astype(BF).astype(F32)
            top_lo = top - top_hi - top_mid
            total_hi = total.astype(BF).astype(F32)
            pieces = [top_hi, top_mid, top_lo, total_hi, total - total_hi]
            for n, piece in enumerate(pieces):
                stats = jnp.where(lane == 8 * h + n, piece, stats)
        colout[i, :, :, 256:384] = stats.astype(BF).reshape(4, 16, HD)

    @pl.loop(0, n_ctx // 4)
    def _(group):
        for member in range(4):
            column_block(group * 4 + member)

    own_back = pltpu.make_async_copy(colout.at[ctx], ret.at[ctx], own_sem.at[1])
    own_back.start()
    for k in range(1, n_ctx):
        j = lax.rem(ctx + k, n_ctx)
        remote(colout.at[j], ret.at[ctx], back_send.at[k - 1], back_recv.at[k - 1], {"ctx": j}).start()

    for copy in w_across:
        copy.wait_recv()
    for copy in w_last + siblings[3:5]:
        copy.start()
    for copy in w_halves:
        copy.wait_recv()
    siblings[5].start()

    own_back.wait()
    for k in range(1, n_ctx):
        source = lax.rem(ctx + n_ctx - k, n_ctx)
        remote(
            ret.at[source], ret.at[source], back_send.at[k - 1], back_recv.at[k - 1], {"ctx": source}
        ).wait_recv()

    @pl.loop(0, rows)
    def _(r):
        stats = ret[:, r, :, 256:384].reshape(cols, HD).astype(F32)
        for h in range(2):
            lanes = slice(h * HD, (h + 1) * HD)
            col_top = stats[:, 8 * h : 8 * h + 1] + stats[:, 8 * h + 1 : 8 * h + 2] + stats[:, 8 * h + 2 : 8 * h + 3]
            col_sum = stats[:, 8 * h + 3 : 8 * h + 4] + stats[:, 8 * h + 4 : 8 * h + 5]
            row_top = maxes[r, :, lanes]
            top = jnp.maximum(row_top, col_top)
            row_scale = jnp.exp(row_top - top)
            col_scale = jnp.exp(col_top - top) * col_sum
            part = ret[:, r, :, lanes].reshape(cols, HD).astype(F32)
            merged = (acc[r, :, lanes] * row_scale + part * col_scale) / (sums[r, :, lanes] * row_scale + col_scale)
            att_ref[pl.ds(pl.multiple_of(r * cols, cols), cols), lanes] = merged.astype(BF)

    for k in range(1, n_ctx):
        source = lax.rem(ctx + n_ctx - k, n_ctx)
        remote(
            recv.at[source], recv.at[source], send_sem.at[k - 1], recv_sem.at[k - 1], {"ctx": source}
        ).wait_send()
        remote(
            ret.at[source], ret.at[source], back_send.at[k - 1], back_recv.at[k - 1], {"ctx": source}
        ).wait_send()
    for copy in w_last:
        copy.wait_recv()
    siblings[6].start()
    for copy in w_first + w_across + w_halves + w_last:
        copy.wait_send()
    for copy in siblings:
        copy.wait()
    own_w.wait()


def mlp_kernel(
    att_ref, tok_ref, wout_ref, gain_ref, wup_ref, wdown_ref, out_ref,
    att, tok, wo, wu, wd, res, normed, act, terms, share, came,
    load_sem, ag_send, ag_recv, rs_send, rs_recv,
):
    chunks, chunk = CHUNKS, 1024 // CHUNKS
    half = chunk // 2
    tp = lax.axis_index("tp")
    here = places(tp)

    barrier = pltpu.get_barrier_semaphore()
    for d in (here.x, here.up, here.down):
        pl.semaphore_signal(barrier, inc=1, device_id={"tp": d}, device_id_type=MESH)
    pl.semaphore_wait(barrier, 3)

    def feats(d):
        return pl.ds(pl.multiple_of(d * 256, 256), 256)

    def rows_of(c):
        return pl.ds(pl.multiple_of(c * chunk, chunk), chunk)

    def low(c):
        return pl.ds(pl.multiple_of(c * chunk, half), half)

    def high(c):
        return pl.ds(pl.multiple_of(c * chunk + half, half), half)

    def gather(kind, c, rows, owner, device):
        place = att.at[rows, feats(owner)]
        source = att_ref.at[rows, :] if kind < 3 else place
        return remote(source, place, ag_send.at[kind, c], ag_recv.at[kind, c], {"tp": device})

    gathers = (
        lambda c: gather(0, c, rows_of(c), tp, here.x),
        lambda c: gather(1, c, rows_of(c), tp, here.up),
        lambda c: gather(2, c, rows_of(c), tp, here.down),
        lambda c: gather(3, c, rows_of(c), here.x, here.up),
        lambda c: gather(4, c, rows_of(c), here.x, here.down),
        lambda c: gather(5, c, low(c), here.down, here.up),
        lambda c: gather(6, c, high(c), here.up, here.down),
        lambda c: gather(7, c, rows_of(c), here.far, here.x),
    )

    def scatter(kind, c, rows, owner, device, slot):
        return remote(
            terms.at[rows, feats(owner)], came.at[slot, rows, :],
            rs_send.at[kind, c], rs_recv.at[kind, c], {"tp": device},
        )

    scatters = (
        lambda c: scatter(0, c, rows_of(c), here.far_x, here.x, 0),
        lambda c: scatter(1, c, rows_of(c), here.up_x, here.up, 1),
        lambda c: scatter(2, c, rows_of(c), here.down_x, here.down, 2),
        lambda c: scatter(3, c, low(c), here.far, here.up, 3),
        lambda c: scatter(4, c, high(c), here.far, here.down, 3),
        lambda c: scatter(5, c, rows_of(c), here.up, here.up, 4),
        lambda c: scatter(6, c, rows_of(c), here.down, here.down, 5),
        lambda c: scatter(7, c, rows_of(c), here.x, here.x, 6),
    )

    def start(copies, kinds, c):
        for kind in kinds:
            copies[kind](c).start()

    def arrive(copies, kinds, c):
        for kind in kinds:
            copies[kind](c).wait_recv()

    def add(rows, owner, slots):
        total = terms[rows, feats(owner)].astype(F32)
        for slot in slots:
            total = total + came[slot, rows, :].astype(F32)
        return total

    def when(c, step):
        @pl.when((c >= 0) & (c < chunks))
        def _():
            step(c)

    def ag_begin(c):
        start(gathers, (0, 1, 2), c)

    def ag_across(c):
        arrive(gathers, (0, 1, 2), c)
        start(gathers, (3, 4, 5, 6), c)

    def ag_far(c):
        arrive(gathers, (5, 6), c)
        start(gathers, (7,), c)

    def ag_end(c):
        arrive(gathers, (3, 4, 7), c)

    def rs_far(c):
        arrive(scatters, (0,), c)
        terms[rows_of(c), feats(here.far)] = add(rows_of(c), here.far, [0]).astype(BF)
        start(scatters, (3, 4), c)

    def rs_across(c):
        arrive(scatters, (1, 2), c)
        terms[rows_of(c), feats(here.x)] = add(rows_of(c), here.x, [1, 2]).astype(BF)
        start(scatters, (7,), c)

    def rs_near(c):
        arrive(scatters, (3,), c)
        terms[low(c), feats(here.up)] = add(low(c), here.up, [3]).astype(BF)
        start(scatters, (5,), c)
        arrive(scatters, (4,), c)
        terms[high(c), feats(here.down)] = add(high(c), here.down, [3]).astype(BF)
        start(scatters, (6,), c)

    def rs_end(c):
        arrive(scatters, (5, 6, 7), c)
        rows = rows_of(c)
        out_ref[rows, :] = (share[rows, :] + add(rows, tp, [4, 5, 6])).astype(BF)

    def compute_up(c):
        rows = rows_of(c)
        for n in range(8):
            cols = slice(n * 256, (n + 1) * 256)
            res[:, cols] = tok[rows, cols].astype(F32) + dot(att[rows, :], wo[:, cols])
        for b in range(chunk // 64):
            part = slice(b * 64, (b + 1) * 64)
            normed[part, :] = layer_norm(res[part, :], gain_ref[...]).astype(BF)
        share[rows, :] = res[:, feats(tp)]
        for n in range(4):
            cols = slice(n * 256, (n + 1) * 256)
            act[:, cols] = jax.nn.gelu(dot(normed[...], wu[:, cols])).astype(BF)

    def compute_down(c):
        rows = rows_of(c)
        order = (here.far_x, here.up_x, here.down_x, here.far, here.x, here.up, here.down, tp)
        for d in order:
            terms[rows, feats(d)] = dot(act[...], wd[:, feats(d)]).astype(BF)
        start(scatters, (0, 1, 2), c)

    for c in range(AHEAD):
        ag_begin(c)
    loads = [
        pltpu.make_async_copy(att_ref, att.at[:, feats(tp)], load_sem.at[0]),
        pltpu.make_async_copy(wout_ref, wo, load_sem.at[1]),
        pltpu.make_async_copy(tok_ref, tok, load_sem.at[2]),
        pltpu.make_async_copy(wup_ref, wu, load_sem.at[3]),
        pltpu.make_async_copy(wdown_ref, wd, load_sem.at[4]),
    ]
    for load in loads:
        load.start()
    ag_across(0)
    ag_across(1)
    ag_far(0)
    for load in loads:
        load.wait()

    @pl.loop(0, chunks + 3)
    def _(c):
        when(c, ag_end)
        when(c, compute_up)
        when(c + AHEAD, ag_begin)
        when(c + 2, ag_across)
        when(c + 1, ag_far)
        when(c - 1, rs_far)
        when(c - 1, rs_across)
        when(c - 2, rs_near)
        when(c - 3, rs_end)
        when(c, compute_down)

    @pl.loop(0, chunks)
    def _(c):
        for copy in gathers + scatters:
            copy(c).wait_send()


ANY = pl.BlockSpec(memory_space=pl.ANY)
VMEM = pl.BlockSpec(memory_space=pltpu.VMEM)
SMEM = pl.BlockSpec(memory_space=pltpu.SMEM)
DMA = pltpu.SemaphoreType.DMA


def on_device(tokens, block_lists, gain_attn, w_qkv, w_out, gain_mlp, w_up, w_down):
    rows, cols, width = tokens.shape
    flat = tokens.reshape(rows * cols, width)
    attended, w_full = pl.pallas_call(
        attn_kernel,
        out_shape=(
            jax.ShapeDtypeStruct((rows * cols, 256), BF),
            jax.ShapeDtypeStruct((width, width), BF),
        ),
        in_specs=[SMEM, ANY, VMEM, ANY, ANY],
        out_specs=(VMEM, ANY),
        scratch_shapes=[
            pltpu.VMEM((4, 256, 2048), BF),
            pltpu.VMEM((3, 2048, 256), BF),
            pltpu.VMEM((256, 2048), BF),
            pltpu.VMEM((4, 256, 768), BF),
            pltpu.VMEM((16, 4, 16, 768), BF),
            pltpu.VMEM((16, 4, 16, 384), BF),
            pltpu.VMEM((16, 4, 16, 384), BF),
            pltpu.VMEM((4, 256, 256), F32),
            pltpu.VMEM((4, 256, 256), F32),
            pltpu.VMEM((4, 256, 256), F32),
            DMA((5,)), DMA((2,)), DMA((15,)), DMA((15,)), DMA((15,)), DMA((15,)),
            DMA((9,)), DMA((9,)), DMA((7,)), DMA((7,)),
        ],
        compiler_params=pltpu.CompilerParams(collective_id=0, has_side_effects=True, vmem_limit_bytes=56 << 20),
        name="attn",
    )(block_lists.T, flat, gain_attn.reshape(1, width), jnp.transpose(w_qkv, (1, 0, 2)), w_out)
    out = pl.pallas_call(
        mlp_kernel,
        out_shape=jax.ShapeDtypeStruct((rows * cols, 256), BF),
        in_specs=[ANY, ANY, ANY, VMEM, ANY, ANY],
        out_specs=VMEM,
        scratch_shapes=[
            pltpu.VMEM((1024, 2048), BF),
            pltpu.VMEM((1024, 2048), BF),
            pltpu.VMEM((2048, 2048), BF),
            pltpu.VMEM((2048, 1024), BF),
            pltpu.VMEM((1024, 2048), BF),
            pltpu.VMEM((1024 // CHUNKS, 2048), F32),
            pltpu.VMEM((1024 // CHUNKS, 2048), BF),
            pltpu.VMEM((1024 // CHUNKS, 1024), BF),
            pltpu.VMEM((1024, 2048), BF),
            pltpu.VMEM((1024, 256), F32),
            pltpu.VMEM((7, 1024, 256), BF),
            DMA((5,)), DMA((8, CHUNKS)), DMA((8, CHUNKS)), DMA((8, CHUNKS)), DMA((8, CHUNKS)),
        ],
        compiler_params=pltpu.CompilerParams(collective_id=1, has_side_effects=True, vmem_limit_bytes=56 << 20),
        name="mlp",
    )(attended, flat, w_full, gain_mlp.reshape(1, width), w_up, w_down)
    return out.reshape(rows, cols, 256)


def solution(mesh):
    return jax.shard_map(
        on_device,
        mesh=mesh,
        in_specs=(
            P("ctx", None, None),
            P(),
            P(),
            P(None, None, "tp"),
            P("tp", None),
            P(),
            P(None, "tp"),
            P("tp", None),
        ),
        out_specs=P("ctx", None, "tp"),
        check_vma=False,
    )
```

```python
import functools

import jax
import jax.numpy as jnp
from jax import lax
from jax.experimental import pallas as pl
from jax.experimental.pallas import tpu as pltpu
from jax.sharding import PartitionSpec as P

HD = 128
MESH = pl.DeviceIdType.MESH
NEG = -1e30
CHUNKS = 4
AHEAD = 3
BF = jnp.bfloat16
F32 = jnp.float32


def remote(src, dst, send_sem, recv_sem, device):
    return pltpu.make_async_remote_copy(
        src_ref=src, dst_ref=dst, send_sem=send_sem, recv_sem=recv_sem, device_id=device, device_id_type=MESH
    )


def layer_norm(values, gain):
    centre = jnp.mean(values, axis=-1, keepdims=True)
    centred = values - centre
    variance = jnp.mean(centred * centred, axis=-1, keepdims=True)
    return centred * lax.rsqrt(variance + 1e-05) * gain


def dot(a, b):
    return jnp.dot(a, b, preferred_element_type=F32)


def dot_t(a, b):
    return lax.dot_general(a, b, (((1,), (1,)), ((), ())), preferred_element_type=F32)


class places:
    def __init__(self, tp):
        def other(d):
            return d + 1 - 2 * lax.rem(d, 2)

        self.x = other(tp)
        self.up, self.down, self.far = (lax.rem(tp + step, 8) for step in (2, 6, 4))
        self.up_x, self.down_x, self.far_x = other(self.up), other(self.down), other(self.far)


def layer_kernel(
    lists, tok_ref, gain_attn_ref, wqkv_ref, wout_ref, gain_mlp_ref, wup_ref, wdown_ref, out_ref,
    tok, wqkv, normed, qkv, recv_0, recv_1, colout, ret, acc, maxes, sums,
    att, wo, wu, wd, res, act, terms, share, came,
    tok_sem, load_sem, own_sem, back_sem, send_sem, recv_sem, back_send, back_recv,
    wo_send, wo_recv, wc_send, wc_recv, ag_send, ag_recv, rs_send, rs_recv,
):
    n_ctx, rows, cols = 16, 4, 256
    recv = (recv_0, recv_1)
    part_cols = cols // n_ctx
    ctx = lax.axis_index("ctx")
    tp = lax.axis_index("tp")
    here = places(tp)
    core = lax.rem(ctx, 2)
    sibling = ctx + 1 - 2 * core

    def feats(d):
        return pl.ds(pl.multiple_of(d * 256, 256), 256)

    def row_tokens(r):
        return pl.ds(pl.multiple_of(r * cols, cols), cols)

    def tok_load(r):
        return pltpu.make_async_copy(tok_ref.at[row_tokens(r), :], tok.at[row_tokens(r), :], tok_sem.at[r])

    wqkv_load = pltpu.make_async_copy(wqkv_ref, wqkv, load_sem.at[0])
    loads = [
        pltpu.make_async_copy(wout_ref, wo.at[feats(tp), :], load_sem.at[1]),
        pltpu.make_async_copy(wup_ref, wu, load_sem.at[2]),
        pltpu.make_async_copy(wdown_ref, wd, load_sem.at[3]),
    ]
    tok_load(0).start()
    wqkv_load.start()
    for r in range(1, rows):
        tok_load(r).start()

    barrier = pltpu.get_barrier_semaphore()
    for k in range(1, n_ctx):
        pl.semaphore_signal(barrier, inc=1, device_id={"ctx": lax.rem(ctx + k, n_ctx)}, device_id_type=MESH)
    for d in (here.x, here.up, here.down):
        pl.semaphore_signal(barrier, inc=1, device_id={"tp": d}, device_id_type=MESH)
    pl.semaphore_wait(barrier, n_ctx - 1 + 3)

    def w_rows(owner, begin=0, size=128):
        return wo.at[pl.ds(pl.multiple_of(owner * 256 + core * 128 + begin, 64), size), :]

    def pass_on(kind, owner, device, begin=0, size=128):
        place = w_rows(owner, begin, size)
        return remote(place, place, wo_send.at[kind], wo_recv.at[kind], {"tp": device})

    own_half = wout_ref.at[pl.ds(pl.multiple_of(core * 128, 128), 128), :]
    w_first = [
        remote(own_half, w_rows(tp), wo_send.at[kind], wo_recv.at[kind], {"tp": device})
        for kind, device in enumerate((here.x, here.up, here.down))
    ]
    w_across = [pass_on(3, here.x, here.up), pass_on(4, here.x, here.down)]
    w_halves = [pass_on(5, here.down, here.up, 0, 64), pass_on(6, here.up, here.down, 64, 64)]
    w_last = [pass_on(7, here.down_x, here.up, 0, 64), pass_on(8, here.up_x, here.down, 64, 64)]

    def to_sibling(kind, owner):
        place = w_rows(owner)
        return remote(place, place, wc_send.at[kind], wc_recv.at[kind], {"ctx": sibling})

    siblings = [
        to_sibling(kind, owner)
        for kind, owner in enumerate((here.x, here.up, here.down, here.up_x, here.down_x, here.far, here.far_x))
    ]
    for copy in w_first:
        copy.start()

    def col_share(j):
        return pl.ds(pl.multiple_of(j * part_cols, part_cols), part_cols)

    def exchange(h, k):
        source = lax.rem(ctx + n_ctx - k, n_ctx)
        place = recv[h].at[source]
        return remote(place, place, send_sem.at[h, k - 1], recv_sem.at[h, k - 1], {"ctx": source})

    def give_back(h, k):
        j = lax.rem(ctx + k, n_ctx)
        return remote(colout.at[h, j], ret.at[h, ctx], back_send.at[h, k - 1], back_recv.at[h, k - 1], {"ctx": j})

    own_blocks = [
        pltpu.make_async_copy(qkv.at[h, :, col_share(ctx), :], recv[h].at[ctx], own_sem.at[h]) for h in range(2)
    ]
    own_backs = [pltpu.make_async_copy(colout.at[h, ctx], ret.at[h, ctx], back_sem.at[h]) for h in range(2)]

    wqkv_load.wait()

    @pl.loop(0, rows)
    def _(r):
        tok_load(r).wait()
        for b in range(cols // 64):
            part = slice(b * 64, (b + 1) * 64)
            tokens = tok[pl.ds(pl.multiple_of(r * cols + b * 64, 64), 64), :]
            normed[part, :] = layer_norm(tokens.astype(F32), gain_attn_ref[...]).astype(BF)
        for n in range(3):
            both = dot(normed[...], wqkv[n]).astype(BF)
            for h in range(2):
                qkv[h, r, :, n * HD : (n + 1) * HD] = both[:, h * HD : (h + 1) * HD]
        for k in range(1, n_ctx):
            j = lax.rem(ctx + k, n_ctx)
            remote(
                qkv.at[0, r, col_share(j), :], recv[0].at[ctx, r],
                send_sem.at[0, k - 1], recv_sem.at[0, k - 1], {"ctx": j},
            ).start()

    for k in range(1, n_ctx):
        j = lax.rem(ctx + k, n_ctx)
        remote(
            qkv.at[1, :, col_share(j), :], recv[1].at[ctx], send_sem.at[1, k - 1], recv_sem.at[1, k - 1], {"ctx": j}
        ).start()
    for copy in own_blocks + loads:
        copy.start()

    causal = lax.broadcasted_iota(jnp.int32, (cols, cols), 1) <= lax.broadcasted_iota(jnp.int32, (cols, cols), 0)

    @pl.loop(0, rows)
    def _(r):
        for h in range(2):
            q, key, val = (qkv[h, r, :, n * HD : (n + 1) * HD] for n in range(3))
            scores = jnp.where(causal, dot_t(q, key) * HD ** (-0.5), NEG)
            top = jnp.max(scores, axis=-1, keepdims=True)
            weights = jnp.exp(scores - top)
            acc[r, :, h * HD : (h + 1) * HD] = dot(weights.astype(BF), val)
            maxes[r, :, h * HD : (h + 1) * HD] = jnp.broadcast_to(top, (cols, HD))
            sums[r, :, h * HD : (h + 1) * HD] = jnp.broadcast_to(jnp.sum(weights, axis=-1, keepdims=True), (cols, HD))

    q_id = lax.broadcasted_iota(jnp.int32, (64, 256), 0)
    k_id = lax.broadcasted_iota(jnp.int32, (64, 256), 1)
    entry = k_id // 64
    same = lax.rem(q_id, 16) == lax.rem(k_id, 16)
    earlier = same & (entry == 0) & (lax.rem(k_id, 64) // 16 < q_id // 16)
    lane = lax.broadcasted_iota(jnp.int32, (64, HD), 1)
    eye = (lax.broadcasted_iota(jnp.int32, (64, HD), 0) == lane).astype(BF)

    def turn(a):
        return lax.dot_general(a, eye[: a.shape[0]], (((0,), (0,)), ((), ())), preferred_element_type=F32)

    def column_block(h, i):
        ids = [lists[l, i] for l in range(4)]
        fresh = []
        for l in range(1, 4):
            new = jnp.int32(1)
            for before in range(l):
                new = new * (ids[l] != ids[before]).astype(jnp.int32)
            fresh.append(new)
        usable = jnp.where(entry == 1, fresh[0], jnp.where(entry == 2, fresh[1], fresh[2]))
        mask = earlier | (same & (entry > 0) & (usable > 0))
        q = recv[h][i, :, :, 0:HD].reshape(64, HD)
        key, val = (
            jnp.concatenate([recv[h][b, :, :, n * HD : (n + 1) * HD].reshape(64, HD) for b in ids], axis=0)
            for n in (1, 2)
        )
        scores = jnp.where(mask, dot_t(q, key) * HD ** (-0.5), NEG)
        top = jnp.max(scores, axis=-1, keepdims=True)
        weights = jnp.where(mask, jnp.exp(scores - top), 0.0)
        total = jnp.sum(weights, axis=-1, keepdims=True)
        colout[h, i, 0:64, :] = (dot(weights.astype(BF), val) / jnp.maximum(total, 1.0)).astype(BF)
        top_hi = top.astype(BF).astype(F32)
        top_mid = (top - top_hi).astype(BF).astype(F32)
        total_hi = total.astype(BF).astype(F32)
        stats = jnp.zeros((64, HD), F32)
        for n, piece in enumerate((top_hi, top_mid, top - top_hi - top_mid, total_hi, total - total_hi)):
            stats = jnp.where(lane == n, piece, stats)
        colout[h, i, 64:80, :] = turn(stats.astype(BF))[0:16, :].astype(BF)

    def column_part(h):
        own_blocks[h].wait()
        for k in range(1, n_ctx):
            exchange(h, k).wait_recv()

        @pl.loop(0, n_ctx // 4)
        def _(group):
            for member in range(4):
                column_block(h, group * 4 + member)

        own_backs[h].start()
        for k in range(1, n_ctx):
            give_back(h, k).start()

    def merge(h, j):
        lanes = slice(h * HD, (h + 1) * HD)
        stats = turn(ret[h, j, 64:80, :])[0:64, :]
        col_top = stats[:, 0:1] + stats[:, 1:2] + stats[:, 2:3]
        col_sum = stats[:, 3:4] + stats[:, 4:5]
        row_top, row_sum, row_part = (a[:, col_share(j), lanes].reshape(64, HD) for a in (maxes, sums, acc))
        top = jnp.maximum(row_top, col_top)
        row_scale = jnp.exp(row_top - top)
        col_scale = jnp.exp(col_top - top) * col_sum
        merged = row_part * row_scale + ret[h, j, 0:64, :].astype(F32) * col_scale
        merged = (merged / (row_sum * row_scale + col_scale)).astype(BF)
        place = pl.ds(pl.multiple_of(tp * 256 + h * HD, HD), HD)
        for r in range(rows):
            att[pl.ds(pl.multiple_of(r * cols + j * part_cols, part_cols), part_cols), place] = merged[
                r * part_cols : (r + 1) * part_cols
            ]

    def merge_part(h):
        own_backs[h].wait()
        for k in range(1, n_ctx):
            give_back(h, k).wait_recv()

        @pl.loop(0, n_ctx // 4)
        def _(group):
            for member in range(4):
                merge(h, group * 4 + member)

    for copy in w_first[1:]:
        copy.wait_recv()
    for copy in w_halves + siblings[1:3]:
        copy.start()
    w_first[0].wait_recv()
    for copy in w_across + siblings[:1]:
        copy.start()
    column_part(0)
    for copy in w_halves:
        copy.wait_recv()
    siblings[5].start()
    column_part(1)
    for copy in w_across:
        copy.wait_recv()
    for copy in w_last + siblings[3:5]:
        copy.start()
    merge_part(0)
    merge_part(1)

    chunks, chunk = CHUNKS, 1024 // CHUNKS
    half = chunk // 2

    def rows_of(c):
        return pl.ds(pl.multiple_of(c * chunk, chunk), chunk)

    def low(c):
        return pl.ds(pl.multiple_of(c * chunk, half), half)

    def high(c):
        return pl.ds(pl.multiple_of(c * chunk + half, half), half)

    def gather(kind, c, rows, owner, device):
        place = att.at[rows, feats(owner)]
        return remote(place, place, ag_send.at[kind, c], ag_recv.at[kind, c], {"tp": device})

    gathers = (
        lambda c: gather(0, c, rows_of(c), tp, here.x),
        lambda c: gather(1, c, rows_of(c), tp, here.up),
        lambda c: gather(2, c, rows_of(c), tp, here.down),
        lambda c: gather(3, c, rows_of(c), here.x, here.up),
        lambda c: gather(4, c, rows_of(c), here.x, here.down),
        lambda c: gather(5, c, low(c), here.down, here.up),
        lambda c: gather(6, c, high(c), here.up, here.down),
        lambda c: gather(7, c, rows_of(c), here.far, here.x),
    )

    def scatter(kind, c, rows, owner, device, slot):
        return remote(
            terms.at[rows, feats(owner)], came.at[slot, rows, :],
            rs_send.at[kind, c], rs_recv.at[kind, c], {"tp": device},
        )

    scatters = (
        lambda c: scatter(0, c, rows_of(c), here.far_x, here.x, 0),
        lambda c: scatter(1, c, rows_of(c), here.up_x, here.up, 1),
        lambda c: scatter(2, c, rows_of(c), here.down_x, here.down, 2),
        lambda c: scatter(3, c, low(c), here.far, here.up, 3),
        lambda c: scatter(4, c, high(c), here.far, here.down, 3),
        lambda c: scatter(5, c, rows_of(c), here.up, here.up, 4),
        lambda c: scatter(6, c, rows_of(c), here.down, here.down, 5),
        lambda c: scatter(7, c, rows_of(c), here.x, here.x, 6),
    )

    def start(copies, kinds, c):
        for kind in kinds:
            copies[kind](c).start()

    def arrive(copies, kinds, c):
        for kind in kinds:
            copies[kind](c).wait_recv()

    def add(rows, owner, slots):
        total = terms[rows, feats(owner)].astype(F32)
        for slot in slots:
            total = total + came[slot, rows, :].astype(F32)
        return total

    def when(c, step):
        @pl.when((c >= 0) & (c < chunks))
        def _():
            step(c)

    def ag_begin(c):
        start(gathers, (0, 1, 2), c)

    def ag_across(c):
        arrive(gathers, (0, 1, 2), c)
        start(gathers, (3, 4, 5, 6), c)

    def ag_far(c):
        arrive(gathers, (5, 6), c)
        start(gathers, (7,), c)

    def ag_end(c):
        arrive(gathers, (3, 4, 7), c)

    def rs_far(c):
        arrive(scatters, (0,), c)
        terms[rows_of(c), feats(here.far)] = add(rows_of(c), here.far, [0]).astype(BF)
        start(scatters, (3, 4), c)

    def rs_across(c):
        arrive(scatters, (1, 2), c)
        terms[rows_of(c), feats(here.x)] = add(rows_of(c), here.x, [1, 2]).astype(BF)
        start(scatters, (7,), c)

    def rs_near(c):
        arrive(scatters, (3,), c)
        terms[low(c), feats(here.up)] = add(low(c), here.up, [3]).astype(BF)
        start(scatters, (5,), c)
        arrive(scatters, (4,), c)
        terms[high(c), feats(here.down)] = add(high(c), here.down, [3]).astype(BF)
        start(scatters, (6,), c)

    def rs_end(c):
        arrive(scatters, (5, 6, 7), c)
        rows = rows_of(c)
        out_ref[rows, :] = (share[rows, :] + add(rows, tp, [4, 5, 6])).astype(BF)

    def compute_up(c):
        rows = rows_of(c)
        for n in range(8):
            cols = slice(n * 256, (n + 1) * 256)
            res[:, cols] = tok[rows, cols].astype(F32) + dot(att[rows, :], wo[:, cols])
        for b in range(chunk // 64):
            part = slice(b * 64, (b + 1) * 64)
            normed[part, :] = layer_norm(res[part, :], gain_mlp_ref[...]).astype(BF)
        share[rows, :] = res[:, feats(tp)]
        for n in range(4):
            cols = slice(n * 256, (n + 1) * 256)
            act[:, cols] = jax.nn.gelu(dot(normed[...], wu[:, cols])).astype(BF)

    def compute_down(c):
        rows = rows_of(c)
        order = (here.far_x, here.up_x, here.down_x, here.far, here.x, here.up, here.down, tp)
        for d in order:
            terms[rows, feats(d)] = dot(act[...], wd[:, feats(d)]).astype(BF)
        start(scatters, (0, 1, 2), c)

    for c in range(AHEAD):
        ag_begin(c)
    ag_across(0)
    ag_across(1)
    ag_far(0)
    for copy in w_last:
        copy.wait_recv()
    siblings[6].start()
    for copy in loads:
        copy.wait()
    for copy in siblings:
        copy.wait_recv()

    @pl.loop(0, chunks + 3)
    def _(c):
        when(c, ag_end)
        when(c, compute_up)
        when(c + AHEAD, ag_begin)
        when(c + 2, ag_across)
        when(c + 1, ag_far)
        when(c - 1, rs_far)
        when(c - 1, rs_across)
        when(c - 2, rs_near)
        when(c - 3, rs_end)
        when(c, compute_down)

    @pl.loop(0, chunks)
    def _(c):
        for copy in gathers + scatters:
            copy(c).wait_send()

    for copy in w_first + w_across + w_halves + w_last + siblings:
        copy.wait_send()
    for h in range(2):
        for k in range(1, n_ctx):
            exchange(h, k).wait_send()
            give_back(h, k).wait_send()


ANY = pl.BlockSpec(memory_space=pl.ANY)
VMEM = pl.BlockSpec(memory_space=pltpu.VMEM)
SMEM = pl.BlockSpec(memory_space=pltpu.SMEM)
DMA = pltpu.SemaphoreType.DMA


def on_device(tokens, block_lists, gain_attn, w_qkv, w_out, gain_mlp, w_up, w_down):
    rows, cols, width = tokens.shape
    flat = tokens.reshape(rows * cols, width)
    out = pl.pallas_call(
        layer_kernel,
        out_shape=jax.ShapeDtypeStruct((rows * cols, 256), BF),
        in_specs=[SMEM, ANY, VMEM, ANY, ANY, VMEM, ANY, ANY],
        out_specs=VMEM,
        scratch_shapes=[
            pltpu.VMEM((1024, 2048), BF),
            pltpu.VMEM((3, 2048, 256), BF),
            pltpu.VMEM((256, 2048), BF),
            pltpu.VMEM((2, 4, 256, 384), BF),
            pltpu.VMEM((16, 4, 16, 384), BF),
            pltpu.VMEM((16, 4, 16, 384), BF),
            pltpu.VMEM((2, 16, 80, 128), BF),
            pltpu.VMEM((2, 16, 80, 128), BF),
            pltpu.VMEM((4, 256, 256), F32),
            pltpu.VMEM((4, 256, 256), F32),
            pltpu.VMEM((4, 256, 256), F32),
            pltpu.VMEM((1024, 2048), BF),
            pltpu.VMEM((2048, 2048), BF),
            pltpu.VMEM((2048, 1024), BF),
            pltpu.VMEM((1024, 2048), BF),
            pltpu.VMEM((1024 // CHUNKS, 2048), F32),
            pltpu.VMEM((1024 // CHUNKS, 1024), BF),
            pltpu.VMEM((1024, 2048), BF),
            pltpu.VMEM((1024, 256), F32),
            pltpu.VMEM((7, 1024, 256), BF),
            DMA((4,)), DMA((4,)), DMA((2,)), DMA((2,)),
            DMA((2, 15)), DMA((2, 15)), DMA((2, 15)), DMA((2, 15)),
            DMA((9,)), DMA((9,)), DMA((7,)), DMA((7,)),
            DMA((8, CHUNKS)), DMA((8, CHUNKS)), DMA((8, CHUNKS)), DMA((8, CHUNKS)),
        ],
        compiler_params=pltpu.CompilerParams(collective_id=0, has_side_effects=True, vmem_limit_bytes=60 << 20),
        name="layer",
    )(
        block_lists.T, flat, gain_attn.reshape(1, width), jnp.transpose(w_qkv, (1, 0, 2)), w_out,
        gain_mlp.reshape(1, width), w_up, w_down,
    )
    return out.reshape(rows, cols, 256)


def solution(mesh):
    return jax.shard_map(
        on_device,
        mesh=mesh,
        in_specs=(
            P("ctx", None, None),
            P(),
            P(),
            P(None, None, "tp"),
            P("tp", None),
            P(),
            P(None, "tp"),
            P("tp", None),
        ),
        out_specs=P("ctx", None, "tp"),
        check_vma=False,
    )
```

```python
import functools

import jax
import jax.numpy as jnp
from jax import lax
from jax.experimental import pallas as pl
from jax.experimental.pallas import tpu as pltpu
from jax.sharding import PartitionSpec as P

HD = 128
MESH = pl.DeviceIdType.MESH
NEG = -1e30
CHUNKS = 4
AHEAD = 3
BF = jnp.bfloat16
F32 = jnp.float32


def remote(src, dst, send_sem, recv_sem, device):
    return pltpu.make_async_remote_copy(
        src_ref=src, dst_ref=dst, send_sem=send_sem, recv_sem=recv_sem, device_id=device, device_id_type=MESH
    )


def layer_norm(values, gain):
    centre = jnp.mean(values, axis=-1, keepdims=True)
    centred = values - centre
    variance = jnp.mean(centred * centred, axis=-1, keepdims=True)
    return centred * lax.rsqrt(variance + 1e-05) * gain


def dot(a, b):
    return jnp.dot(a, b, preferred_element_type=F32)


def dot_t(a, b):
    return lax.dot_general(a, b, (((1,), (1,)), ((), ())), preferred_element_type=F32)


class places:
    def __init__(self, tp):
        def other(d):
            return d + 1 - 2 * lax.rem(d, 2)

        self.x = other(tp)
        self.up, self.down, self.far = (lax.rem(tp + step, 8) for step in (2, 6, 4))
        self.up_x, self.down_x, self.far_x = other(self.up), other(self.down), other(self.far)


def layer_kernel(
    lists, tok_ref, gain_attn_ref, wqkv_ref, wout_ref, gain_mlp_ref, wup_ref, wdown_ref, out_ref,
    tok, wqkv, normed, qkv, recv_0, recv_1, colout, ret, acc, maxes, sums,
    att, wo, wu, wd, res, act, terms, share, came,
    tok_sem, load_sem, own_sem, back_sem, send_sem, recv_sem, back_send, back_recv,
    wo_send, wo_recv, wc_send, wc_recv, ag_send, ag_recv, rs_send, rs_recv,
):
    n_ctx, rows, cols = 16, 4, 256
    recv = (recv_0, recv_1)
    part_cols = cols // n_ctx
    ctx = lax.axis_index("ctx")
    tp = lax.axis_index("tp")
    here = places(tp)
    core = lax.rem(ctx, 2)
    sibling = ctx + 1 - 2 * core

    def feats(d):
        return pl.ds(pl.multiple_of(d * 256, 256), 256)

    def row_tokens(r):
        return pl.ds(pl.multiple_of(r * cols, cols), cols)

    def tok_load(r):
        return pltpu.make_async_copy(tok_ref.at[row_tokens(r), :], tok.at[row_tokens(r), :], tok_sem.at[r])

    wqkv_load = pltpu.make_async_copy(wqkv_ref, wqkv, load_sem.at[0])
    loads = [
        pltpu.make_async_copy(wout_ref, wo.at[feats(tp), :], load_sem.at[1]),
        pltpu.make_async_copy(wup_ref, wu, load_sem.at[2]),
        pltpu.make_async_copy(wdown_ref, wd, load_sem.at[3]),
    ]
    tok_load(0).start()
    wqkv_load.start()
    for r in range(1, rows):
        tok_load(r).start()

    beside = {"ctx": ctx + 2 - 4 * lax.rem(ctx // 2, 2), "tp": here.x}
    up, down = {"tp": here.up}, {"tp": here.down}

    barrier = pltpu.get_barrier_semaphore()
    for k in range(1, n_ctx):
        pl.semaphore_signal(barrier, inc=1, device_id={"ctx": lax.rem(ctx + k, n_ctx)}, device_id_type=MESH)
    for d in (here.x, here.up, here.down):
        pl.semaphore_signal(barrier, inc=1, device_id={"tp": d}, device_id_type=MESH)
    pl.semaphore_signal(barrier, inc=1, device_id=beside, device_id_type=MESH)
    pl.semaphore_wait(barrier, n_ctx - 1 + 4)

    def w_rows(owner, begin=0, size=64):
        return pl.ds(pl.multiple_of(owner * 256 + core * 128 + begin, 64), size)

    def w_send(kind, owner, piece, device):
        place = wo.at[w_rows(owner, 64 * piece), :]
        source = wout_ref.at[pl.ds(pl.multiple_of(core * 128 + 64 * piece, 64), 64), :] if kind < 6 else place
        return remote(source, place, wo_send.at[kind], wo_recv.at[kind], device)

    w_up = [w_send(0, tp, 0, up), w_send(1, tp, 1, up)]
    w_down = [w_send(2, tp, 1, down), w_send(3, tp, 0, down)]
    w_beside = [w_send(4, tp, 0, beside), w_send(5, tp, 1, beside)]
    w_onward = [w_send(6, here.down, 0, up), w_send(7, here.up, 1, down)]
    w_across = [[w_send(8 + 2 * p, here.x, p, up), w_send(9 + 2 * p, here.x, p, down)] for p in range(2)]
    w_far = [w_send(12, here.far, 0, beside), w_send(13, here.far, 1, beside)]
    w_all = w_up + w_down + w_beside + w_onward + w_across[0] + w_across[1] + w_far

    def to_sibling(kind, owner):
        place = wo.at[w_rows(owner, 0, 128), :]
        return remote(place, place, wc_send.at[kind], wc_recv.at[kind], {"ctx": sibling})

    siblings = [
        to_sibling(kind, owner)
        for kind, owner in enumerate((here.x, here.up, here.down, here.up_x, here.down_x, here.far, here.far_x))
    ]

    def start_all(copies):
        for copy in copies:
            copy.start()

    def arrive_all(copies):
        for copy in copies:
            copy.wait_recv()

    start_all([w_up[0], w_down[0], w_beside[0], w_up[1], w_down[1], w_beside[1]])

    def col_share(j):
        return pl.ds(pl.multiple_of(j * part_cols, part_cols), part_cols)

    def exchange(h, k):
        source = lax.rem(ctx + n_ctx - k, n_ctx)
        place = recv[h].at[source]
        return remote(place, place, send_sem.at[h, k - 1], recv_sem.at[h, k - 1], {"ctx": source})

    def give_back(h, k):
        j = lax.rem(ctx + k, n_ctx)
        return remote(colout.at[h, j], ret.at[h, ctx], back_send.at[h, k - 1], back_recv.at[h, k - 1], {"ctx": j})

    own_blocks = [
        pltpu.make_async_copy(qkv.at[h, :, col_share(ctx), :], recv[h].at[ctx], own_sem.at[h]) for h in range(2)
    ]
    own_backs = [pltpu.make_async_copy(colout.at[h, ctx], ret.at[h, ctx], back_sem.at[h]) for h in range(2)]

    wqkv_load.wait()

    @pl.loop(0, rows)
    def _(r):
        tok_load(r).wait()
        for b in range(cols // 64):
            part = slice(b * 64, (b + 1) * 64)
            tokens = tok[pl.ds(pl.multiple_of(r * cols + b * 64, 64), 64), :]
            normed[part, :] = layer_norm(tokens.astype(F32), gain_attn_ref[...]).astype(BF)
        for n in range(3):
            both = dot(normed[...], wqkv[n]).astype(BF)
            for h in range(2):
                qkv[h, r, :, n * HD : (n + 1) * HD] = both[:, h * HD : (h + 1) * HD]
        for k in range(1, n_ctx):
            j = lax.rem(ctx + k, n_ctx)
            remote(
                qkv.at[0, r, col_share(j), :], recv[0].at[ctx, r],
                send_sem.at[0, k - 1], recv_sem.at[0, k - 1], {"ctx": j},
            ).start()

    for k in range(1, n_ctx):
        j = lax.rem(ctx + k, n_ctx)
        remote(
            qkv.at[1, :, col_share(j), :], recv[1].at[ctx], send_sem.at[1, k - 1], recv_sem.at[1, k - 1], {"ctx": j}
        ).start()
    for copy in own_blocks + loads:
        copy.start()

    arrive_all([w_up[0], w_down[0]])
    start_all(w_onward)
    arrive_all([w_beside[0]])
    start_all(w_across[0])

    causal = lax.broadcasted_iota(jnp.int32, (cols, cols), 1) <= lax.broadcasted_iota(jnp.int32, (cols, cols), 0)

    @pl.loop(0, rows)
    def _(r):
        for h in range(2):
            q, key, val = (qkv[h, r, :, n * HD : (n + 1) * HD] for n in range(3))
            scores = jnp.where(causal, dot_t(q, key) * HD ** (-0.5), NEG)
            top = jnp.max(scores, axis=-1, keepdims=True)
            weights = jnp.exp(scores - top)
            acc[r, :, h * HD : (h + 1) * HD] = dot(weights.astype(BF), val)
            maxes[r, :, h * HD : (h + 1) * HD] = jnp.broadcast_to(top, (cols, HD))
            sums[r, :, h * HD : (h + 1) * HD] = jnp.broadcast_to(jnp.sum(weights, axis=-1, keepdims=True), (cols, HD))

    q_id = lax.broadcasted_iota(jnp.int32, (64, 256), 0)
    k_id = lax.broadcasted_iota(jnp.int32, (64, 256), 1)
    entry = k_id // 64
    same = lax.rem(q_id, 16) == lax.rem(k_id, 16)
    earlier = same & (entry == 0) & (lax.rem(k_id, 64) // 16 < q_id // 16)
    lane = lax.broadcasted_iota(jnp.int32, (64, HD), 1)
    eye = (lax.broadcasted_iota(jnp.int32, (64, HD), 0) == lane).astype(BF)

    def turn(a):
        return lax.dot_general(a, eye[: a.shape[0]], (((0,), (0,)), ((), ())), preferred_element_type=F32)

    def column_block(h, i):
        ids = [lists[l, i] for l in range(4)]
        fresh = []
        for l in range(1, 4):
            new = jnp.int32(1)
            for before in range(l):
                new = new * (ids[l] != ids[before]).astype(jnp.int32)
            fresh.append(new)
        usable = jnp.where(entry == 1, fresh[0], jnp.where(entry == 2, fresh[1], fresh[2]))
        mask = earlier | (same & (entry > 0) & (usable > 0))
        q = recv[h][i, :, :, 0:HD].reshape(64, HD)
        key, val = (
            jnp.concatenate([recv[h][b, :, :, n * HD : (n + 1) * HD].reshape(64, HD) for b in ids], axis=0)
            for n in (1, 2)
        )
        scores = jnp.where(mask, dot_t(q, key) * HD ** (-0.5), NEG)
        top = jnp.max(scores, axis=-1, keepdims=True)
        weights = jnp.where(mask, jnp.exp(scores - top), 0.0)
        total = jnp.sum(weights, axis=-1, keepdims=True)
        colout[h, i, 0:64, :] = (dot(weights.astype(BF), val) / jnp.maximum(total, 1.0)).astype(BF)
        top_hi = top.astype(BF).astype(F32)
        top_mid = (top - top_hi).astype(BF).astype(F32)
        total_hi = total.astype(BF).astype(F32)
        stats = jnp.zeros((64, HD), F32)
        for n, piece in enumerate((top_hi, top_mid, top - top_hi - top_mid, total_hi, total - total_hi)):
            stats = jnp.where(lane == n, piece, stats)
        colout[h, i, 64:80, :] = turn(stats.astype(BF))[0:16, :].astype(BF)

    def column_part(h):
        own_blocks[h].wait()
        for k in range(1, n_ctx):
            exchange(h, k).wait_recv()

        @pl.loop(0, n_ctx // 4)
        def _(group):
            for member in range(4):
                column_block(h, group * 4 + member)

        own_backs[h].start()
        for k in range(1, n_ctx):
            give_back(h, k).start()

    def merge(h, j):
        lanes = slice(h * HD, (h + 1) * HD)
        stats = turn(ret[h, j, 64:80, :])[0:64, :]
        col_top = stats[:, 0:1] + stats[:, 1:2] + stats[:, 2:3]
        col_sum = stats[:, 3:4] + stats[:, 4:5]
        row_top, row_sum, row_part = (a[:, col_share(j), lanes].reshape(64, HD) for a in (maxes, sums, acc))
        top = jnp.maximum(row_top, col_top)
        row_scale = jnp.exp(row_top - top)
        col_scale = jnp.exp(col_top - top) * col_sum
        merged = row_part * row_scale + ret[h, j, 0:64, :].astype(F32) * col_scale
        merged = (merged / (row_sum * row_scale + col_scale)).astype(BF)
        place = pl.ds(pl.multiple_of(tp * 256 + h * HD, HD), HD)
        for r in range(rows):
            att[pl.ds(pl.multiple_of(r * cols + j * part_cols, part_cols), part_cols), place] = merged[
                r * part_cols : (r + 1) * part_cols
            ]

    def merge_part(h):
        own_backs[h].wait()
        for k in range(1, n_ctx):
            give_back(h, k).wait_recv()

        @pl.loop(0, n_ctx // 4)
        def _(group):
            for member in range(4):
                merge(h, group * 4 + member)

    arrive_all([w_beside[1]])
    start_all(w_across[1])
    arrive_all([w_up[1], w_down[1]])
    start_all(siblings[:3])
    column_part(0)
    arrive_all(w_onward)
    start_all(w_far)
    start_all(siblings[5:6])
    column_part(1)
    arrive_all(w_across[0] + w_across[1])
    start_all(siblings[3:5])
    merge_part(0)
    merge_part(1)

    chunks, chunk = CHUNKS, 1024 // CHUNKS
    half = chunk // 2

    def rows_of(c):
        return pl.ds(pl.multiple_of(c * chunk, chunk), chunk)

    def low(c):
        return pl.ds(pl.multiple_of(c * chunk, half), half)

    def high(c):
        return pl.ds(pl.multiple_of(c * chunk + half, half), half)

    def gather(kind, c, rows, owner, device):
        place = att.at[rows, feats(owner)]
        return remote(place, place, ag_send.at[kind, c], ag_recv.at[kind, c], {"tp": device})

    gathers = (
        lambda c: gather(0, c, rows_of(c), tp, here.x),
        lambda c: gather(1, c, rows_of(c), tp, here.up),
        lambda c: gather(2, c, rows_of(c), tp, here.down),
        lambda c: gather(3, c, rows_of(c), here.x, here.up),
        lambda c: gather(4, c, rows_of(c), here.x, here.down),
        lambda c: gather(5, c, low(c), here.down, here.up),
        lambda c: gather(6, c, high(c), here.up, here.down),
        lambda c: gather(7, c, rows_of(c), here.far, here.x),
    )

    def scatter(kind, c, rows, owner, device, slot):
        return remote(
            terms.at[rows, feats(owner)], came.at[slot, rows, :],
            rs_send.at[kind, c], rs_recv.at[kind, c], {"tp": device},
        )

    scatters = (
        lambda c: scatter(0, c, rows_of(c), here.far_x, here.x, 0),
        lambda c: scatter(1, c, rows_of(c), here.up_x, here.up, 1),
        lambda c: scatter(2, c, rows_of(c), here.down_x, here.down, 2),
        lambda c: scatter(3, c, low(c), here.far, here.up, 3),
        lambda c: scatter(4, c, high(c), here.far, here.down, 3),
        lambda c: scatter(5, c, rows_of(c), here.up, here.up, 4),
        lambda c: scatter(6, c, rows_of(c), here.down, here.down, 5),
        lambda c: scatter(7, c, rows_of(c), here.x, here.x, 6),
    )

    def start(copies, kinds, c):
        for kind in kinds:
            copies[kind](c).start()

    def arrive(copies, kinds, c):
        for kind in kinds:
            copies[kind](c).wait_recv()

    def add(rows, owner, slots):
        total = terms[rows, feats(owner)].astype(F32)
        for slot in slots:
            total = total + came[slot, rows, :].astype(F32)
        return total

    def when(c, step):
        @pl.when((c >= 0) & (c < chunks))
        def _():
            step(c)

    def ag_begin(c):
        start(gathers, (0, 1, 2), c)

    def ag_across(c):
        arrive(gathers, (0, 1, 2), c)
        start(gathers, (3, 4, 5, 6), c)

    def ag_far(c):
        arrive(gathers, (5, 6), c)
        start(gathers, (7,), c)

    def ag_end(c):
        arrive(gathers, (3, 4, 7), c)

    def rs_far(c):
        arrive(scatters, (0,), c)
        terms[rows_of(c), feats(here.far)] = add(rows_of(c), here.far, [0]).astype(BF)
        start(scatters, (3, 4), c)

    def rs_across(c):
        arrive(scatters, (1, 2), c)
        terms[rows_of(c), feats(here.x)] = add(rows_of(c), here.x, [1, 2]).astype(BF)
        start(scatters, (7,), c)

    def rs_near(c):
        arrive(scatters, (3,), c)
        terms[low(c), feats(here.up)] = add(low(c), here.up, [3]).astype(BF)
        start(scatters, (5,), c)
        arrive(scatters, (4,), c)
        terms[high(c), feats(here.down)] = add(high(c), here.down, [3]).astype(BF)
        start(scatters, (6,), c)

    def rs_end(c):
        arrive(scatters, (5, 6, 7), c)
        rows = rows_of(c)
        out_ref[rows, :] = (share[rows, :] + add(rows, tp, [4, 5, 6])).astype(BF)

    def compute_up(c):
        rows = rows_of(c)
        for n in range(8):
            cols = slice(n * 256, (n + 1) * 256)
            res[:, cols] = tok[rows, cols].astype(F32) + dot(att[rows, :], wo[:, cols])
        for b in range(chunk // 64):
            part = slice(b * 64, (b + 1) * 64)
            normed[part, :] = layer_norm(res[part, :], gain_mlp_ref[...]).astype(BF)
        share[rows, :] = res[:, feats(tp)]
        for n in range(4):
            cols = slice(n * 256, (n + 1) * 256)
            act[:, cols] = jax.nn.gelu(dot(normed[0:chunk, :], wu[:, cols])).astype(BF)

    def compute_down(c):
        rows = rows_of(c)
        order = (here.far_x, here.up_x, here.down_x, here.far, here.x, here.up, here.down, tp)
        for d in order:
            terms[rows, feats(d)] = dot(act[...], wd[:, feats(d)]).astype(BF)
        start(scatters, (0, 1, 2), c)

    for c in range(AHEAD):
        ag_begin(c)
    ag_across(0)
    ag_across(1)
    ag_far(0)
    arrive_all(w_far)
    start_all(siblings[6:])
    for copy in loads:
        copy.wait()
    arrive_all(siblings)

    @pl.loop(0, chunks + 3)
    def _(c):
        when(c, ag_end)
        when(c + AHEAD, ag_begin)
        when(c + 2, ag_across)
        when(c + 1, ag_far)
        when(c, compute_up)
        when(c - 1, rs_far)
        when(c, compute_down)
        when(c - 1, rs_across)
        when(c - 2, rs_near)
        when(c - 3, rs_end)

    @pl.loop(0, chunks)
    def _(c):
        for copy in gathers + scatters:
            copy(c).wait_send()

    for copy in w_all + siblings:
        copy.wait_send()
    for h in range(2):
        for k in range(1, n_ctx):
            exchange(h, k).wait_send()
            give_back(h, k).wait_send()


ANY = pl.BlockSpec(memory_space=pl.ANY)
VMEM = pl.BlockSpec(memory_space=pltpu.VMEM)
SMEM = pl.BlockSpec(memory_space=pltpu.SMEM)
DMA = pltpu.SemaphoreType.DMA


def on_device(tokens, block_lists, gain_attn, w_qkv, w_out, gain_mlp, w_up, w_down):
    rows, cols, width = tokens.shape
    flat = tokens.reshape(rows * cols, width)
    out = pl.pallas_call(
        layer_kernel,
        out_shape=jax.ShapeDtypeStruct((rows * cols, 256), BF),
        in_specs=[SMEM, ANY, VMEM, ANY, ANY, VMEM, ANY, ANY],
        out_specs=VMEM,
        scratch_shapes=[
            pltpu.VMEM((1024, 2048), BF),
            pltpu.VMEM((3, 2048, 256), BF),
            pltpu.VMEM((256, 2048), BF),
            pltpu.VMEM((2, 4, 256, 384), BF),
            pltpu.VMEM((16, 4, 16, 384), BF),
            pltpu.VMEM((16, 4, 16, 384), BF),
            pltpu.VMEM((2, 16, 80, 128), BF),
            pltpu.VMEM((2, 16, 80, 128), BF),
            pltpu.VMEM((4, 256, 256), F32),
            pltpu.VMEM((4, 256, 256), F32),
            pltpu.VMEM((4, 256, 256), F32),
            pltpu.VMEM((1024, 2048), BF),
            pltpu.VMEM((2048, 2048), BF),
            pltpu.VMEM((2048, 1024), BF),
            pltpu.VMEM((1024, 2048), BF),
            pltpu.VMEM((1024 // CHUNKS, 2048), F32),
            pltpu.VMEM((1024 // CHUNKS, 1024), BF),
            pltpu.VMEM((1024, 2048), BF),
            pltpu.VMEM((1024, 256), F32),
            pltpu.VMEM((7, 1024, 256), BF),
            DMA((4,)), DMA((4,)), DMA((2,)), DMA((2,)),
            DMA((2, 15)), DMA((2, 15)), DMA((2, 15)), DMA((2, 15)),
            DMA((14,)), DMA((14,)), DMA((7,)), DMA((7,)),
            DMA((8, CHUNKS)), DMA((8, CHUNKS)), DMA((8, CHUNKS)), DMA((8, CHUNKS)),
        ],
        compiler_params=pltpu.CompilerParams(collective_id=0, has_side_effects=True, vmem_limit_bytes=60 << 20),
        name="layer",
    )(
        block_lists.T, flat, gain_attn.reshape(1, width), jnp.transpose(w_qkv, (1, 0, 2)), w_out,
        gain_mlp.reshape(1, width), w_up, w_down,
    )
    return out.reshape(rows, cols, 256)


def solution(mesh):
    return jax.shard_map(
        on_device,
        mesh=mesh,
        in_specs=(
            P("ctx", None, None),
            P(),
            P(),
            P(None, None, "tp"),
            P("tp", None),
            P(),
            P(None, "tp"),
            P("tp", None),
        ),
        out_specs=P("ctx", None, "tp"),
        check_vma=False,
    )
```

```python
import functools

import jax
import jax.numpy as jnp
from jax import lax
from jax.experimental import pallas as pl
from jax.experimental.pallas import tpu as pltpu
from jax.sharding import PartitionSpec as P

HD = 128
MESH = pl.DeviceIdType.MESH
NEG = -1e30
CHUNKS = 4
AHEAD = 3
BF = jnp.bfloat16
F32 = jnp.float32


def remote(src, dst, send_sem, recv_sem, device):
    return pltpu.make_async_remote_copy(
        src_ref=src, dst_ref=dst, send_sem=send_sem, recv_sem=recv_sem, device_id=device, device_id_type=MESH
    )


def layer_norm(values, gain):
    centre = jnp.mean(values, axis=-1, keepdims=True)
    centred = values - centre
    variance = jnp.mean(centred * centred, axis=-1, keepdims=True)
    return centred * lax.rsqrt(variance + 1e-05) * gain


def dot(a, b):
    return jnp.dot(a, b, preferred_element_type=F32)


def dot_t(a, b):
    return lax.dot_general(a, b, (((1,), (1,)), ((), ())), preferred_element_type=F32)


class places:
    def __init__(self, tp):
        def other(d):
            return d + 1 - 2 * lax.rem(d, 2)

        self.x = other(tp)
        self.up, self.down, self.far = (lax.rem(tp + step, 8) for step in (2, 6, 4))
        self.up_x, self.down_x, self.far_x = other(self.up), other(self.down), other(self.far)


def layer_kernel(
    lists, tok_ref, gain_attn_ref, wqkv_ref, wout_ref, gain_mlp_ref, wup_ref, wdown_ref, out_ref,
    tok, wqkv, normed, qkv, recv_0, recv_1, colout, ret, acc, maxes, sums,
    att, wo, wu, wd, res, act, terms, share, came,
    tok_sem, load_sem, own_sem, back_sem, send_sem, recv_sem, back_send, back_recv,
    wo_send, wo_recv, wc_send, wc_recv, ag_send, ag_recv, rs_send, rs_recv,
):
    n_ctx, rows, cols = 16, 4, 256
    recv = (recv_0, recv_1)
    part_cols = cols // n_ctx
    ctx = lax.axis_index("ctx")
    tp = lax.axis_index("tp")
    here = places(tp)
    core = lax.rem(ctx, 2)
    sibling = ctx + 1 - 2 * core

    def feats(d):
        return pl.ds(pl.multiple_of(d * 256, 256), 256)

    def row_tokens(r):
        return pl.ds(pl.multiple_of(r * cols, cols), cols)

    def head_lanes(h):
        return pl.ds(pl.multiple_of(tp * 256 + h * HD, HD), HD)

    def tok_load(r):
        return pltpu.make_async_copy(tok_ref.at[row_tokens(r), :], tok.at[row_tokens(r), :], tok_sem.at[r])

    wqkv_load = pltpu.make_async_copy(wqkv_ref, wqkv, load_sem.at[0])
    loads = [
        pltpu.make_async_copy(wout_ref, wo.at[feats(tp), :], load_sem.at[1]),
        pltpu.make_async_copy(wup_ref, wu, load_sem.at[2]),
        pltpu.make_async_copy(wdown_ref, wd, load_sem.at[3]),
    ]
    tok_load(0).start()
    wqkv_load.start()
    for r in range(1, rows):
        tok_load(r).start()

    beside = {"ctx": ctx + 2 - 4 * lax.rem(ctx // 2, 2), "tp": here.x}
    up, down = {"tp": here.up}, {"tp": here.down}

    barrier = pltpu.get_barrier_semaphore()
    for k in range(1, n_ctx):
        pl.semaphore_signal(barrier, inc=1, device_id={"ctx": lax.rem(ctx + k, n_ctx)}, device_id_type=MESH)
    for d in (here.x, here.up, here.down):
        pl.semaphore_signal(barrier, inc=1, device_id={"tp": d}, device_id_type=MESH)
    pl.semaphore_signal(barrier, inc=1, device_id=beside, device_id_type=MESH)

    def norm(r):
        for b in range(cols // 64):
            part = slice(b * 64, (b + 1) * 64)
            tokens = tok[pl.ds(pl.multiple_of(r * cols + b * 64, 64), 64), :]
            normed[lax.rem(r, 2), part, :] = layer_norm(tokens.astype(F32), gain_attn_ref[...]).astype(BF)

    tok_load(0).wait()
    norm(0)
    pl.semaphore_wait(barrier, n_ctx - 1 + 4)

    def w_rows(owner, begin=0, size=64):
        return pl.ds(pl.multiple_of(owner * 256 + core * 128 + begin, 64), size)

    def w_send(kind, owner, piece, device):
        place = wo.at[w_rows(owner, 64 * piece), :]
        source = wout_ref.at[pl.ds(pl.multiple_of(core * 128 + 64 * piece, 64), 64), :] if kind < 6 else place
        return remote(source, place, wo_send.at[kind], wo_recv.at[kind], device)

    w_up = [w_send(0, tp, 0, up), w_send(1, tp, 1, up)]
    w_down = [w_send(2, tp, 1, down), w_send(3, tp, 0, down)]
    w_beside = [w_send(4, tp, 0, beside), w_send(5, tp, 1, beside)]
    w_onward = [w_send(6, here.down, 0, up), w_send(7, here.up, 1, down)]
    w_across = [w_send(8, here.x, 0, down), w_send(9, here.x, 1, up)]
    w_near = [w_send(10, here.down, 0, beside), w_send(11, here.up, 1, beside)]
    w_far = [w_send(12, here.far, 0, beside), w_send(13, here.far, 1, beside)]
    w_all = w_up + w_down + w_beside + w_onward + w_across + w_near + w_far

    def to_sibling(kind, owner):
        place = wo.at[w_rows(owner, 0, 128), :]
        return remote(place, place, wc_send.at[kind], wc_recv.at[kind], {"ctx": sibling})

    siblings = [
        to_sibling(kind, owner)
        for kind, owner in enumerate((here.x, here.up, here.down, here.up_x, here.down_x, here.far, here.far_x))
    ]

    def start_all(copies):
        for copy in copies:
            copy.start()

    def arrive_all(copies):
        for copy in copies:
            copy.wait_recv()

    start_all([w_up[0], w_down[0], w_beside[0], w_up[1], w_down[1], w_beside[1]])

    def col_share(j):
        return pl.ds(pl.multiple_of(j * part_cols, part_cols), part_cols)

    def exchange(h, k):
        source = lax.rem(ctx + n_ctx - k, n_ctx)
        place = recv[h].at[source]
        return remote(place, place, send_sem.at[h, k - 1], recv_sem.at[h, k - 1], {"ctx": source})

    def give_back(h, k):
        j = lax.rem(ctx + k, n_ctx)
        return remote(colout.at[h, j], ret.at[h, ctx], back_send.at[h, k], back_recv.at[h, k], {"ctx": j})

    own_blocks = [
        pltpu.make_async_copy(qkv.at[h, :, col_share(ctx), :], recv[h].at[ctx], own_sem.at[h]) for h in range(2)
    ]
    own_backs = [pltpu.make_async_copy(colout.at[h, ctx], ret.at[h, ctx], back_sem.at[h]) for h in range(2)]

    wqkv_load.wait()
    for r in range(1, rows):
        tok_load(r).wait()

    @pl.loop(0, rows)
    def _(r):
        norm(jnp.minimum(r + 1, rows - 1))
        for n in range(3):
            both = dot(normed[lax.rem(r, 2)], wqkv[n]).astype(BF)
            for h in range(2):
                qkv[h, r, :, n * HD : (n + 1) * HD] = both[:, h * HD : (h + 1) * HD]
        for k in range(1, n_ctx):
            j = lax.rem(ctx + k, n_ctx)
            remote(
                qkv.at[0, r, col_share(j), :], recv[0].at[ctx, r],
                send_sem.at[0, k - 1], recv_sem.at[0, k - 1], {"ctx": j},
            ).start()

    for k in range(1, n_ctx):
        j = lax.rem(ctx + k, n_ctx)
        remote(
            qkv.at[1, :, col_share(j), :], recv[1].at[ctx], send_sem.at[1, k - 1], recv_sem.at[1, k - 1], {"ctx": j}
        ).start()
    for copy in own_blocks + loads:
        copy.start()

    arrive_all([w_up[0], w_down[0]])
    start_all(w_onward + w_near)
    arrive_all([w_beside[0]])
    start_all(w_across[:1])

    causal = lax.broadcasted_iota(jnp.int32, (cols, cols), 1) <= lax.broadcasted_iota(jnp.int32, (cols, cols), 0)

    @pl.loop(0, rows)
    def _(r):
        for h in range(2):
            q, key, val = (qkv[h, r, :, n * HD : (n + 1) * HD] for n in range(3))
            scores = jnp.where(causal, dot_t(q, key) * HD ** (-0.5), NEG)
            top = jnp.max(scores, axis=-1, keepdims=True)
            weights = jnp.exp(scores - top)
            acc[r, :, h * HD : (h + 1) * HD] = dot(weights.astype(BF), val)
            maxes[r, :, h * HD : (h + 1) * HD] = jnp.broadcast_to(top, (cols, HD))
            sums[r, :, h * HD : (h + 1) * HD] = jnp.broadcast_to(jnp.sum(weights, axis=-1, keepdims=True), (cols, HD))

    q_id = lax.broadcasted_iota(jnp.int32, (64, 256), 0)
    k_id = lax.broadcasted_iota(jnp.int32, (64, 256), 1)
    entry = k_id // 64
    same = lax.rem(q_id, 16) == lax.rem(k_id, 16)
    earlier = same & (entry == 0) & (lax.rem(k_id, 64) // 16 < q_id // 16)
    lane = lax.broadcasted_iota(jnp.int32, (64, HD), 1)
    eye = (lax.broadcasted_iota(jnp.int32, (64, HD), 0) == lane).astype(BF)

    def turn(a):
        return lax.dot_general(a, eye[: a.shape[0]], (((0,), (0,)), ((), ())), preferred_element_type=F32)

    def column_block(h, i):
        ids = [lists[l, i] for l in range(4)]
        fresh = []
        for l in range(1, 4):
            new = jnp.int32(1)
            for before in range(l):
                new = new * (ids[l] != ids[before]).astype(jnp.int32)
            fresh.append(new)
        usable = jnp.where(entry == 1, fresh[0], jnp.where(entry == 2, fresh[1], fresh[2]))
        mask = earlier | (same & (entry > 0) & (usable > 0))
        q = recv[h][i, :, :, 0:HD].reshape(64, HD)
        key, val = (
            jnp.concatenate([recv[h][b, :, :, n * HD : (n + 1) * HD].reshape(64, HD) for b in ids], axis=0)
            for n in (1, 2)
        )
        scores = jnp.where(mask, dot_t(q, key) * HD ** (-0.5), NEG)
        top = jnp.max(scores, axis=-1, keepdims=True)
        weights = jnp.where(mask, jnp.exp(scores - top), 0.0)
        total = jnp.sum(weights, axis=-1, keepdims=True)
        colout[h, i, 0:64, :] = (dot(weights.astype(BF), val) / jnp.maximum(total, 1.0)).astype(BF)
        top_hi = top.astype(BF).astype(F32)
        top_mid = (top - top_hi).astype(BF).astype(F32)
        total_hi = total.astype(BF).astype(F32)
        stats = jnp.zeros((64, HD), F32)
        for n, piece in enumerate((top_hi, top_mid, top - top_hi - top_mid, total_hi, total - total_hi)):
            stats = jnp.where(lane == n, piece, stats)
        colout[h, i, 64:80, :] = turn(stats.astype(BF))[0:16, :].astype(BF)

    def column_part(h):
        own_blocks[h].wait()
        for k in range(1, n_ctx):
            exchange(h, k).wait_recv()

        @pl.loop(0, n_ctx // 4)
        def _(group):
            for member in range(4):
                column_block(h, lax.rem(ctx + group * 4 + member, n_ctx))
            for member in range(4):
                k = group * 4 + member

                @pl.when(k == 0)
                def _():
                    own_backs[h].start()

                @pl.when(k > 0)
                def _():
                    give_back(h, k).start()

    def merge(h, j):
        lanes = slice(h * HD, (h + 1) * HD)
        stats = turn(ret[h, j, 64:80, :])[0:64, :]
        col_top = stats[:, 0:1] + stats[:, 1:2] + stats[:, 2:3]
        col_sum = stats[:, 3:4] + stats[:, 4:5]
        row_top, row_sum, row_part = (a[:, col_share(j), lanes].reshape(64, HD) for a in (maxes, sums, acc))
        top = jnp.maximum(row_top, col_top)
        row_scale = jnp.exp(row_top - top)
        col_scale = jnp.exp(col_top - top) * col_sum
        merged = row_part * row_scale + ret[h, j, 0:64, :].astype(F32) * col_scale
        merged = (merged / (row_sum * row_scale + col_scale)).astype(BF)
        for r in range(rows):
            att[pl.ds(pl.multiple_of(r * cols + j * part_cols, part_cols), part_cols), head_lanes(h)] = merged[
                r * part_cols : (r + 1) * part_cols
            ]

    def merge_part(h):
        @pl.loop(0, n_ctx // 4)
        def _(group):
            for member in range(4):
                k = group * 4 + member

                @pl.when(k == 0)
                def _():
                    own_backs[h].wait()

                @pl.when(k > 0)
                def _():
                    give_back(h, k).wait_recv()

            for member in range(4):
                merge(h, lax.rem(ctx + n_ctx - group * 4 - member, n_ctx))

    arrive_all([w_beside[1]])
    start_all(w_across[1:])
    arrive_all([w_up[1], w_down[1]])
    start_all(siblings[:3])
    column_part(0)
    arrive_all(w_onward)
    start_all(w_far)
    start_all(siblings[5:6])
    column_part(1)
    arrive_all(w_across + w_near)
    start_all(siblings[3:5])
    chunks, chunk = CHUNKS, 1024 // CHUNKS
    half = chunk // 2

    def rows_of(c):
        return pl.ds(pl.multiple_of(c * chunk, chunk), chunk)

    def low(c):
        return pl.ds(pl.multiple_of(c * chunk, half), half)

    def high(c):
        return pl.ds(pl.multiple_of(c * chunk + half, half), half)

    def gather(kind, c, rows, owner, device, lanes=None):
        place = att.at[rows, feats(owner) if lanes is None else lanes]
        return remote(place, place, ag_send.at[kind, c], ag_recv.at[kind, c], {"tp": device})

    gathers = (
        lambda c: gather(0, c, rows_of(c), tp, here.x),
        lambda c: gather(1, c, rows_of(c), tp, here.up, head_lanes(0)),
        lambda c: gather(2, c, rows_of(c), tp, here.down, head_lanes(0)),
        lambda c: gather(3, c, rows_of(c), here.x, here.up),
        lambda c: gather(4, c, rows_of(c), here.x, here.down),
        lambda c: gather(5, c, low(c), here.down, here.up),
        lambda c: gather(6, c, high(c), here.up, here.down),
        lambda c: gather(7, c, rows_of(c), here.far, here.x),
        lambda c: gather(8, c, rows_of(c), tp, here.up, head_lanes(1)),
        lambda c: gather(9, c, rows_of(c), tp, here.down, head_lanes(1)),
    )

    def scatter(kind, c, rows, owner, device, slot):
        return remote(
            terms.at[rows, feats(owner)], came.at[slot, rows, :],
            rs_send.at[kind, c], rs_recv.at[kind, c], {"tp": device},
        )

    scatters = (
        lambda c: scatter(0, c, rows_of(c), here.far_x, here.x, 0),
        lambda c: scatter(1, c, rows_of(c), here.up_x, here.up, 1),
        lambda c: scatter(2, c, rows_of(c), here.down_x, here.down, 2),
        lambda c: scatter(3, c, low(c), here.far, here.up, 3),
        lambda c: scatter(4, c, high(c), here.far, here.down, 3),
        lambda c: scatter(5, c, rows_of(c), here.up, here.up, 4),
        lambda c: scatter(6, c, rows_of(c), here.down, here.down, 5),
        lambda c: scatter(7, c, rows_of(c), here.x, here.x, 6),
    )

    def start(copies, kinds, c):
        for kind in kinds:
            copies[kind](c).start()

    def arrive(copies, kinds, c):
        for kind in kinds:
            copies[kind](c).wait_recv()

    def add(rows, owner, slots):
        total = terms[rows, feats(owner)].astype(F32)
        for slot in slots:
            total = total + came[slot, rows, :].astype(F32)
        return total

    def when(c, step):
        @pl.when((c >= 0) & (c < chunks))
        def _():
            step(c)

    def ag_begin(c):
        start(gathers, (8, 9, 0), c)

    def ag_across(c):
        arrive(gathers, (0, 1, 2, 8, 9), c)
        start(gathers, (3, 4, 5, 6), c)

    def ag_far(c):
        arrive(gathers, (5, 6), c)
        start(gathers, (7,), c)

    def ag_end(c):
        arrive(gathers, (3, 4, 7), c)

    def rs_far(c):
        arrive(scatters, (0,), c)
        terms[rows_of(c), feats(here.far)] = add(rows_of(c), here.far, [0]).astype(BF)
        start(scatters, (3, 4), c)

    def rs_across(c):
        arrive(scatters, (1, 2), c)
        terms[rows_of(c), feats(here.x)] = add(rows_of(c), here.x, [1, 2]).astype(BF)
        start(scatters, (7,), c)

    def rs_near(c):
        arrive(scatters, (3,), c)
        terms[low(c), feats(here.up)] = add(low(c), here.up, [3]).astype(BF)
        start(scatters, (5,), c)
        arrive(scatters, (4,), c)
        terms[high(c), feats(here.down)] = add(high(c), here.down, [3]).astype(BF)
        start(scatters, (6,), c)

    def rs_end(c):
        arrive(scatters, (5, 6, 7), c)
        rows = rows_of(c)
        out_ref[rows, :] = (share[rows, :] + add(rows, tp, [4, 5, 6])).astype(BF)

    def compute_up(c):
        rows = rows_of(c)
        for n in range(8):
            cols = slice(n * 256, (n + 1) * 256)
            res[:, cols] = tok[rows, cols].astype(F32) + dot(att[rows, :], wo[:, cols])
        for b in range(chunk // 64):
            part = slice(b * 64, (b + 1) * 64)
            normed[0, part, :] = layer_norm(res[part, :], gain_mlp_ref[...]).astype(BF)
        share[rows, :] = res[:, feats(tp)]
        for n in range(4):
            cols = slice(n * 256, (n + 1) * 256)
            act[:, cols] = jax.nn.gelu(dot(normed[0, 0:chunk, :], wu[:, cols])).astype(BF)

    def compute_down(c):
        rows = rows_of(c)
        order = (here.far_x, here.up_x, here.down_x, here.far, here.x, here.up, here.down, tp)
        for d in order:
            terms[rows, feats(d)] = dot(act[...], wd[:, feats(d)]).astype(BF)
        start(scatters, (0, 1, 2), c)

    merge_part(0)
    for c in range(chunks):
        start(gathers, (1, 2), c)
    merge_part(1)
    for c in range(AHEAD):
        ag_begin(c)
    ag_across(0)
    ag_across(1)
    ag_far(0)
    arrive_all(w_far)
    start_all(siblings[6:])
    for copy in loads:
        copy.wait()
    arrive_all(siblings)

    @pl.loop(0, chunks + 3)
    def _(c):
        when(c, ag_end)
        when(c + AHEAD, ag_begin)
        when(c + 2, ag_across)
        when(c + 1, ag_far)
        when(c, compute_up)
        when(c - 1, rs_far)
        when(c, compute_down)
        when(c - 1, rs_across)
        when(c - 2, rs_near)
        when(c - 3, rs_end)

    @pl.loop(0, chunks)
    def _(c):
        for copy in gathers + scatters:
            copy(c).wait_send()

    for copy in w_all + siblings:
        copy.wait_send()
    for h in range(2):
        for k in range(1, n_ctx):
            exchange(h, k).wait_send()
            give_back(h, k).wait_send()


ANY = pl.BlockSpec(memory_space=pl.ANY)
VMEM = pl.BlockSpec(memory_space=pltpu.VMEM)
SMEM = pl.BlockSpec(memory_space=pltpu.SMEM)
DMA = pltpu.SemaphoreType.DMA


def on_device(tokens, block_lists, gain_attn, w_qkv, w_out, gain_mlp, w_up, w_down):
    rows, cols, width = tokens.shape
    flat = tokens.reshape(rows * cols, width)
    out = pl.pallas_call(
        layer_kernel,
        out_shape=jax.ShapeDtypeStruct((rows * cols, 256), BF),
        in_specs=[SMEM, ANY, VMEM, ANY, ANY, VMEM, ANY, ANY],
        out_specs=VMEM,
        scratch_shapes=[
            pltpu.VMEM((1024, 2048), BF),
            pltpu.VMEM((3, 2048, 256), BF),
            pltpu.VMEM((2, 256, 2048), BF),
            pltpu.VMEM((2, 4, 256, 384), BF),
            pltpu.VMEM((16, 4, 16, 384), BF),
            pltpu.VMEM((16, 4, 16, 384), BF),
            pltpu.VMEM((2, 16, 80, 128), BF),
            pltpu.VMEM((2, 16, 80, 128), BF),
            pltpu.VMEM((4, 256, 256), F32),
            pltpu.VMEM((4, 256, 256), F32),
            pltpu.VMEM((4, 256, 256), F32),
            pltpu.VMEM((1024, 2048), BF),
            pltpu.VMEM((2048, 2048), BF),
            pltpu.VMEM((2048, 1024), BF),
            pltpu.VMEM((1024, 2048), BF),
            pltpu.VMEM((1024 // CHUNKS, 2048), F32),
            pltpu.VMEM((1024 // CHUNKS, 1024), BF),
            pltpu.VMEM((1024, 2048), BF),
            pltpu.VMEM((1024, 256), F32),
            pltpu.VMEM((7, 1024, 256), BF),
            DMA((4,)), DMA((4,)), DMA((2,)), DMA((2,)),
            DMA((2, 15)), DMA((2, 15)), DMA((2, 16)), DMA((2, 16)),
            DMA((14,)), DMA((14,)), DMA((7,)), DMA((7,)),
            DMA((10, CHUNKS)), DMA((10, CHUNKS)), DMA((8, CHUNKS)), DMA((8, CHUNKS)),
        ],
        compiler_params=pltpu.CompilerParams(collective_id=0, has_side_effects=True, vmem_limit_bytes=60 << 20),
        name="layer",
    )(
        block_lists.T, flat, gain_attn.reshape(1, width), jnp.transpose(w_qkv, (1, 0, 2)), w_out,
        gain_mlp.reshape(1, width), w_up, w_down,
    )
    return out.reshape(rows, cols, 256)


def solution(mesh):
    return jax.shard_map(
        on_device,
        mesh=mesh,
        in_specs=(
            P("ctx", None, None),
            P(),
            P(),
            P(None, None, "tp"),
            P("tp", None),
            P(),
            P(None, "tp"),
            P("tp", None),
        ),
        out_specs=P("ctx", None, "tp"),
        check_vma=False,
    )
```

```python
import functools

import jax
import jax.numpy as jnp
from jax import lax
from jax.experimental import pallas as pl
from jax.experimental.pallas import tpu as pltpu
from jax.sharding import PartitionSpec as P

HD = 128
MESH = pl.DeviceIdType.MESH
NEG = -1e30
CHUNKS = 4
AHEAD = 3
BF = jnp.bfloat16
F32 = jnp.float32


def remote(src, dst, send_sem, recv_sem, device):
    return pltpu.make_async_remote_copy(
        src_ref=src, dst_ref=dst, send_sem=send_sem, recv_sem=recv_sem, device_id=device, device_id_type=MESH
    )


def layer_norm(values, gain):
    centre = jnp.mean(values, axis=-1, keepdims=True)
    centred = values - centre
    variance = jnp.mean(centred * centred, axis=-1, keepdims=True)
    return centred * lax.rsqrt(variance + 1e-05) * gain


def dot(a, b):
    return jnp.dot(a, b, preferred_element_type=F32)


def dot_t(a, b):
    return lax.dot_general(a, b, (((1,), (1,)), ((), ())), preferred_element_type=F32)


class places:
    def __init__(self, tp):
        def other(d):
            return d + 1 - 2 * lax.rem(d, 2)

        self.x = other(tp)
        self.up, self.down, self.far = (lax.rem(tp + step, 8) for step in (2, 6, 4))
        self.up_x, self.down_x, self.far_x = other(self.up), other(self.down), other(self.far)


def layer_kernel(
    lists, tok_ref, gain_attn_ref, wqkv_ref, wout_ref, gain_mlp_ref, wup_ref, wdown_ref, out_ref,
    tok, wqkv, normed, qkv, recv_0, recv_1, colout, ret, acc, maxes, sums,
    att, wo, wu, wd, res, act, terms, share, came,
    tok_sem, load_sem, own_sem, back_sem, send_sem, recv_sem, back_send, back_recv,
    wo_send, wo_recv, wc_send, wc_recv, ag_send, ag_recv, rs_send, rs_recv,
):
    n_ctx, rows, cols = 16, 4, 256
    recv = (recv_0, recv_1)
    part_cols = cols // n_ctx
    ctx = lax.axis_index("ctx")
    tp = lax.axis_index("tp")
    here = places(tp)
    core = lax.rem(ctx, 2)
    sibling = ctx + 1 - 2 * core

    def feats(d):
        return pl.ds(pl.multiple_of(d * 256, 256), 256)

    def row_tokens(r):
        return pl.ds(pl.multiple_of(r * cols, cols), cols)

    def head_lanes(h):
        return pl.ds(pl.multiple_of(tp * 256 + h * HD, HD), HD)

    def tok_load(r):
        return pltpu.make_async_copy(tok_ref.at[row_tokens(r), :], tok.at[row_tokens(r), :], tok_sem.at[r])

    wqkv_load = pltpu.make_async_copy(wqkv_ref, wqkv, load_sem.at[0])
    loads = [
        pltpu.make_async_copy(wout_ref, wo.at[feats(tp), :], load_sem.at[1]),
        pltpu.make_async_copy(wup_ref, wu, load_sem.at[2]),
        pltpu.make_async_copy(wdown_ref, wd, load_sem.at[3]),
    ]
    tok_load(0).start()
    wqkv_load.start()
    for r in range(1, rows):
        tok_load(r).start()

    beside = {"ctx": ctx + 2 - 4 * lax.rem(ctx // 2, 2), "tp": here.x}
    up, down = {"tp": here.up}, {"tp": here.down}

    barrier = pltpu.get_barrier_semaphore()
    for k in range(1, n_ctx):
        pl.semaphore_signal(barrier, inc=1, device_id={"ctx": lax.rem(ctx + k, n_ctx)}, device_id_type=MESH)
    for d in (here.x, here.up, here.down):
        pl.semaphore_signal(barrier, inc=1, device_id={"tp": d}, device_id_type=MESH)
    pl.semaphore_signal(barrier, inc=1, device_id=beside, device_id_type=MESH)

    def norm(r):
        for b in range(cols // 64):
            part = slice(b * 64, (b + 1) * 64)
            tokens = tok[pl.ds(pl.multiple_of(r * cols + b * 64, 64), 64), :]
            normed[lax.rem(r, 2), part, :] = layer_norm(tokens.astype(F32), gain_attn_ref[...]).astype(BF)

    tok_load(0).wait()
    norm(0)
    pl.semaphore_wait(barrier, n_ctx - 1 + 4)

    def w_rows(owner, begin=0, size=64):
        return pl.ds(pl.multiple_of(owner * 256 + core * 128 + begin, 64), size)

    def w_send(kind, owner, piece, device):
        place = wo.at[w_rows(owner, 64 * piece), :]
        source = wout_ref.at[pl.ds(pl.multiple_of(core * 128 + 64 * piece, 64), 64), :] if kind < 6 else place
        return remote(source, place, wo_send.at[kind], wo_recv.at[kind], device)

    w_up = [w_send(0, tp, 0, up), w_send(1, tp, 1, up)]
    w_down = [w_send(2, tp, 1, down), w_send(3, tp, 0, down)]
    w_beside = [w_send(4, tp, 0, beside), w_send(5, tp, 1, beside)]
    w_onward = [w_send(6, here.down, 0, up), w_send(7, here.up, 1, down)]
    w_across = [w_send(8, here.x, 0, down), w_send(9, here.x, 1, up)]
    w_near = [w_send(10, here.down, 0, beside), w_send(11, here.up, 1, beside)]
    w_far = [w_send(12, here.far, 0, beside), w_send(13, here.far, 1, beside)]
    w_all = w_up + w_down + w_beside + w_onward + w_across + w_near + w_far

    def to_sibling(kind, owner):
        place = wo.at[w_rows(owner, 0, 128), :]
        return remote(place, place, wc_send.at[kind], wc_recv.at[kind], {"ctx": sibling})

    siblings = [
        to_sibling(kind, owner)
        for kind, owner in enumerate((here.x, here.up, here.down, here.up_x, here.down_x, here.far, here.far_x))
    ]

    def start_all(copies):
        for copy in copies:
            copy.start()

    def arrive_all(copies):
        for copy in copies:
            copy.wait_recv()

    start_all([w_up[0], w_down[0], w_beside[0], w_up[1], w_down[1], w_beside[1]])

    def col_share(j):
        return pl.ds(pl.multiple_of(j * part_cols, part_cols), part_cols)

    def exchange(h, k):
        source = lax.rem(ctx + n_ctx - k, n_ctx)
        place = recv[h].at[source]
        return remote(place, place, send_sem.at[h, k - 1], recv_sem.at[h, k - 1], {"ctx": source})

    def give_back(h, k):
        j = lax.rem(ctx + k, n_ctx)
        return remote(colout.at[h, j], ret.at[h, ctx], back_send.at[h, k], back_recv.at[h, k], {"ctx": j})

    own_blocks = [
        pltpu.make_async_copy(qkv.at[h, :, col_share(ctx), :], recv[h].at[ctx], own_sem.at[h]) for h in range(2)
    ]
    own_backs = [pltpu.make_async_copy(colout.at[h, ctx], ret.at[h, ctx], back_sem.at[h]) for h in range(2)]

    wqkv_load.wait()
    for r in range(1, rows):
        tok_load(r).wait()

    @pl.loop(0, rows)
    def _(r):
        norm(jnp.minimum(r + 1, rows - 1))
        for n in range(3):
            both = dot(normed[lax.rem(r, 2)], wqkv[n]).astype(BF)
            for h in range(2):
                qkv[h, r, :, n * HD : (n + 1) * HD] = both[:, h * HD : (h + 1) * HD]
        for k in range(1, n_ctx):
            j = lax.rem(ctx + k, n_ctx)
            remote(
                qkv.at[0, r, col_share(j), :], recv[0].at[ctx, r],
                send_sem.at[0, k - 1], recv_sem.at[0, k - 1], {"ctx": j},
            ).start()

    for k in range(1, n_ctx):
        j = lax.rem(ctx + k, n_ctx)
        remote(
            qkv.at[1, :, col_share(j), :], recv[1].at[ctx], send_sem.at[1, k - 1], recv_sem.at[1, k - 1], {"ctx": j}
        ).start()
    for copy in own_blocks + loads:
        copy.start()

    arrive_all([w_up[0], w_down[0]])
    start_all(w_onward + w_near)
    arrive_all([w_beside[0]])
    start_all(w_across[:1])

    causal = lax.broadcasted_iota(jnp.int32, (cols, cols), 1) <= lax.broadcasted_iota(jnp.int32, (cols, cols), 0)

    @pl.loop(0, rows)
    def _(r):
        for h in range(2):
            q, key, val = (qkv[h, r, :, n * HD : (n + 1) * HD] for n in range(3))
            scores = jnp.where(causal, dot_t(q, key) * HD ** (-0.5), NEG)
            top = jnp.max(scores, axis=-1, keepdims=True)
            weights = jnp.exp(scores - top)
            acc[r, :, h * HD : (h + 1) * HD] = dot(weights.astype(BF), val)
            maxes[r, :, h * HD : (h + 1) * HD] = jnp.broadcast_to(top, (cols, HD))
            sums[r, :, h * HD : (h + 1) * HD] = jnp.broadcast_to(jnp.sum(weights, axis=-1, keepdims=True), (cols, HD))

    q_id = lax.broadcasted_iota(jnp.int32, (64, 256), 0)
    k_id = lax.broadcasted_iota(jnp.int32, (64, 256), 1)
    entry = k_id // 64
    same = lax.rem(q_id, 16) == lax.rem(k_id, 16)
    earlier = same & (entry == 0) & (lax.rem(k_id, 64) // 16 < q_id // 16)
    lane = lax.broadcasted_iota(jnp.int32, (64, HD), 1)
    eye = (lax.broadcasted_iota(jnp.int32, (64, HD), 0) == lane).astype(BF)

    def turn(a):
        return lax.dot_general(a, eye[: a.shape[0]], (((0,), (0,)), ((), ())), preferred_element_type=F32)

    def column_block(h, i):
        ids = [lists[l, i] for l in range(4)]
        fresh = []
        for l in range(1, 4):
            new = jnp.int32(1)
            for before in range(l):
                new = new * (ids[l] != ids[before]).astype(jnp.int32)
            fresh.append(new)
        usable = jnp.where(entry == 1, fresh[0], jnp.where(entry == 2, fresh[1], fresh[2]))
        mask = earlier | (same & (entry > 0) & (usable > 0))
        q = recv[h][i, :, :, 0:HD].reshape(64, HD)
        key, val = (
            jnp.concatenate([recv[h][b, :, :, n * HD : (n + 1) * HD].reshape(64, HD) for b in ids], axis=0)
            for n in (1, 2)
        )
        scores = jnp.where(mask, dot_t(q, key) * HD ** (-0.5), NEG)
        top = jnp.max(scores, axis=-1, keepdims=True)
        weights = jnp.where(mask, jnp.exp(scores - top), 0.0)
        total = jnp.sum(weights, axis=-1, keepdims=True)
        colout[h, i, 0:64, :] = (dot(weights.astype(BF), val) / jnp.maximum(total, 1.0)).astype(BF)
        top_hi = top.astype(BF).astype(F32)
        top_mid = (top - top_hi).astype(BF).astype(F32)
        total_hi = total.astype(BF).astype(F32)
        stats = jnp.zeros((64, HD), F32)
        for n, piece in enumerate((top_hi, top_mid, top - top_hi - top_mid, total_hi, total - total_hi)):
            stats = jnp.where(lane == n, piece, stats)
        colout[h, i, 64:80, :] = turn(stats.astype(BF))[0:16, :].astype(BF)

    def column_part(h):
        own_blocks[h].wait()
        for k in range(1, n_ctx):
            exchange(h, k).wait_recv()

        @pl.loop(0, n_ctx // 8)
        def _(group):
            for member in range(8):
                column_block(h, lax.rem(ctx + group * 8 + member, n_ctx))
            for member in range(8):
                k = group * 8 + member

                @pl.when(k == 0)
                def _():
                    own_backs[h].start()

                @pl.when(k > 0)
                def _():
                    give_back(h, k).start()

    def merge(h, j):
        lanes = slice(h * HD, (h + 1) * HD)
        stats = turn(ret[h, j, 64:80, :])[0:64, :]
        col_top = stats[:, 0:1] + stats[:, 1:2] + stats[:, 2:3]
        col_sum = stats[:, 3:4] + stats[:, 4:5]
        row_top, row_sum, row_part = (a[:, col_share(j), lanes].reshape(64, HD) for a in (maxes, sums, acc))
        top = jnp.maximum(row_top, col_top)
        row_scale = jnp.exp(row_top - top)
        col_scale = jnp.exp(col_top - top) * col_sum
        merged = row_part * row_scale + ret[h, j, 0:64, :].astype(F32) * col_scale
        merged = (merged / (row_sum * row_scale + col_scale)).astype(BF)
        for r in range(rows):
            att[pl.ds(pl.multiple_of(r * cols + j * part_cols, part_cols), part_cols), head_lanes(h)] = merged[
                r * part_cols : (r + 1) * part_cols
            ]

    def merge_part(h):
        @pl.loop(0, n_ctx // 8)
        def _(group):
            for member in range(8):
                k = group * 8 + member

                @pl.when(k == 0)
                def _():
                    own_backs[h].wait()

                @pl.when(k > 0)
                def _():
                    give_back(h, k).wait_recv()

            for member in range(8):
                merge(h, lax.rem(ctx + n_ctx - group * 8 - member, n_ctx))

    arrive_all([w_beside[1]])
    start_all(w_across[1:])
    arrive_all([w_up[1], w_down[1]])
    start_all(siblings[:3])
    column_part(0)
    arrive_all(w_onward)
    start_all(w_far)
    start_all(siblings[5:6])
    column_part(1)
    arrive_all(w_across + w_near)
    start_all(siblings[3:5])
    chunks, chunk = CHUNKS, 1024 // CHUNKS
    half = chunk // 2

    def rows_of(c):
        return pl.ds(pl.multiple_of(c * chunk, chunk), chunk)

    def low(c):
        return pl.ds(pl.multiple_of(c * chunk, half), half)

    def high(c):
        return pl.ds(pl.multiple_of(c * chunk + half, half), half)

    def gather(kind, c, rows, owner, device, lanes=None):
        place = att.at[rows, feats(owner) if lanes is None else lanes]
        return remote(place, place, ag_send.at[kind, c], ag_recv.at[kind, c], {"tp": device})

    gathers = (
        lambda c: gather(0, c, rows_of(c), tp, here.x),
        lambda c: gather(1, c, rows_of(c), tp, here.up, head_lanes(0)),
        lambda c: gather(2, c, rows_of(c), tp, here.down, head_lanes(0)),
        lambda c: gather(3, c, rows_of(c), here.x, here.up),
        lambda c: gather(4, c, rows_of(c), here.x, here.down),
        lambda c: gather(5, c, low(c), here.down, here.up),
        lambda c: gather(6, c, high(c), here.up, here.down),
        lambda c: gather(7, c, rows_of(c), here.far, here.x),
        lambda c: gather(8, c, rows_of(c), tp, here.up, head_lanes(1)),
        lambda c: gather(9, c, rows_of(c), tp, here.down, head_lanes(1)),
    )

    def scatter(kind, c, rows, owner, device, slot):
        return remote(
            terms.at[rows, feats(owner)], came.at[slot, rows, :],
            rs_send.at[kind, c], rs_recv.at[kind, c], {"tp": device},
        )

    scatters = (
        lambda c: scatter(0, c, rows_of(c), here.far_x, here.x, 0),
        lambda c: scatter(1, c, rows_of(c), here.up_x, here.up, 1),
        lambda c: scatter(2, c, rows_of(c), here.down_x, here.down, 2),
        lambda c: scatter(3, c, low(c), here.far, here.up, 3),
        lambda c: scatter(4, c, high(c), here.far, here.down, 3),
        lambda c: scatter(5, c, rows_of(c), here.up, here.up, 4),
        lambda c: scatter(6, c, rows_of(c), here.down, here.down, 5),
        lambda c: scatter(7, c, rows_of(c), here.x, here.x, 6),
    )

    def start(copies, kinds, c):
        for kind in kinds:
            copies[kind](c).start()

    def arrive(copies, kinds, c):
        for kind in kinds:
            copies[kind](c).wait_recv()

    def add(rows, owner, slots):
        total = terms[rows, feats(owner)].astype(F32)
        for slot in slots:
            total = total + came[slot, rows, :].astype(F32)
        return total

    def when(c, step):
        @pl.when((c >= 0) & (c < chunks))
        def _():
            step(c)

    def ag_begin(c):
        start(gathers, (8, 9, 0), c)

    def ag_across(c):
        arrive(gathers, (0, 1, 2, 8, 9), c)
        start(gathers, (3, 5, 4, 6), c)

    def ag_far(c):
        arrive(gathers, (5, 6), c)
        start(gathers, (7,), c)

    def ag_end(c):
        arrive(gathers, (3, 4, 7), c)

    def rs_far(c):
        arrive(scatters, (0,), c)
        terms[rows_of(c), feats(here.far)] = add(rows_of(c), here.far, [0]).astype(BF)
        start(scatters, (3, 4), c)

    def rs_across(c):
        arrive(scatters, (1, 2), c)
        terms[rows_of(c), feats(here.x)] = add(rows_of(c), here.x, [1, 2]).astype(BF)
        start(scatters, (7,), c)

    def rs_near(c):
        arrive(scatters, (3,), c)
        terms[low(c), feats(here.up)] = add(low(c), here.up, [3]).astype(BF)
        start(scatters, (5,), c)
        arrive(scatters, (4,), c)
        terms[high(c), feats(here.down)] = add(high(c), here.down, [3]).astype(BF)
        start(scatters, (6,), c)

    def rs_end(c):
        arrive(scatters, (5, 6, 7), c)
        rows = rows_of(c)
        out_ref[rows, :] = (share[rows, :] + add(rows, tp, [4, 5, 6])).astype(BF)

    def compute_up(c):
        rows = rows_of(c)
        for n in range(8):
            cols = slice(n * 256, (n + 1) * 256)
            res[:, cols] = tok[rows, cols].astype(F32) + dot(att[rows, :], wo[:, cols])
        for b in range(chunk // 64):
            part = slice(b * 64, (b + 1) * 64)
            normed[0, part, :] = layer_norm(res[part, :], gain_mlp_ref[...]).astype(BF)
        share[rows, :] = res[:, feats(tp)]
        for n in range(4):
            cols = slice(n * 256, (n + 1) * 256)
            act[:, cols] = jax.nn.gelu(dot(normed[0, 0:chunk, :], wu[:, cols])).astype(BF)

    def compute_down(c):
        rows = rows_of(c)
        order = (here.far_x, here.up_x, here.down_x, here.far, here.x, here.up, here.down, tp)
        for d in order:
            terms[rows, feats(d)] = dot(act[...], wd[:, feats(d)]).astype(BF)
        start(scatters, (0, 1, 2), c)

    merge_part(0)
    for c in range(chunks):
        start(gathers, (1, 2), c)
    merge_part(1)
    for c in range(AHEAD):
        ag_begin(c)
    ag_across(0)
    ag_across(1)
    ag_far(0)
    arrive_all(w_far)
    start_all(siblings[6:])
    for copy in loads:
        copy.wait()
    arrive_all(siblings)

    @pl.loop(0, chunks)
    def _(c):
        when(c, ag_end)
        when(c + AHEAD, ag_begin)
        when(c + 2, ag_across)
        when(c + 1, ag_far)
        when(c, compute_up)
        when(c - 1, rs_far)
        when(c, compute_down)
        when(c - 1, rs_across)
        when(c - 2, rs_near)
        when(c - 3, rs_end)

    rs_far(3)
    rs_near(2)
    rs_across(3)
    rs_near(3)
    rs_end(1)
    rs_end(2)
    rs_end(3)

    @pl.loop(0, chunks)
    def _(c):
        for copy in gathers + scatters:
            copy(c).wait_send()

    for copy in w_all + siblings:
        copy.wait_send()
    for h in range(2):
        for k in range(1, n_ctx):
            exchange(h, k).wait_send()
            give_back(h, k).wait_send()


ANY = pl.BlockSpec(memory_space=pl.ANY)
VMEM = pl.BlockSpec(memory_space=pltpu.VMEM)
SMEM = pl.BlockSpec(memory_space=pltpu.SMEM)
DMA = pltpu.SemaphoreType.DMA


def on_device(tokens, block_lists, gain_attn, w_qkv, w_out, gain_mlp, w_up, w_down):
    rows, cols, width = tokens.shape
    flat = tokens.reshape(rows * cols, width)
    out = pl.pallas_call(
        layer_kernel,
        out_shape=jax.ShapeDtypeStruct((rows * cols, 256), BF),
        in_specs=[SMEM, ANY, VMEM, ANY, ANY, VMEM, ANY, ANY],
        out_specs=VMEM,
        scratch_shapes=[
            pltpu.VMEM((1024, 2048), BF),
            pltpu.VMEM((3, 2048, 256), BF),
            pltpu.VMEM((2, 256, 2048), BF),
            pltpu.VMEM((2, 4, 256, 384), BF),
            pltpu.VMEM((16, 4, 16, 384), BF),
            pltpu.VMEM((16, 4, 16, 384), BF),
            pltpu.VMEM((2, 16, 80, 128), BF),
            pltpu.VMEM((2, 16, 80, 128), BF),
            pltpu.VMEM((4, 256, 256), F32),
            pltpu.VMEM((4, 256, 256), F32),
            pltpu.VMEM((4, 256, 256), F32),
            pltpu.VMEM((1024, 2048), BF),
            pltpu.VMEM((2048, 2048), BF),
            pltpu.VMEM((2048, 1024), BF),
            pltpu.VMEM((1024, 2048), BF),
            pltpu.VMEM((1024 // CHUNKS, 2048), F32),
            pltpu.VMEM((1024 // CHUNKS, 1024), BF),
            pltpu.VMEM((1024, 2048), BF),
            pltpu.VMEM((1024, 256), F32),
            pltpu.VMEM((7, 1024, 256), BF),
            DMA((4,)), DMA((4,)), DMA((2,)), DMA((2,)),
            DMA((2, 15)), DMA((2, 15)), DMA((2, 16)), DMA((2, 16)),
            DMA((14,)), DMA((14,)), DMA((7,)), DMA((7,)),
            DMA((10, CHUNKS)), DMA((10, CHUNKS)), DMA((8, CHUNKS)), DMA((8, CHUNKS)),
        ],
        compiler_params=pltpu.CompilerParams(collective_id=0, has_side_effects=True, vmem_limit_bytes=60 << 20),
        name="layer",
    )(
        block_lists.T, flat, gain_attn.reshape(1, width), jnp.transpose(w_qkv, (1, 0, 2)), w_out,
        gain_mlp.reshape(1, width), w_up, w_down,
    )
    return out.reshape(rows, cols, 256)


def solution(mesh):
    return jax.shard_map(
        on_device,
        mesh=mesh,
        in_specs=(
            P("ctx", None, None),
            P(),
            P(),
            P(None, None, "tp"),
            P("tp", None),
            P(),
            P(None, "tp"),
            P("tp", None),
        ),
        out_specs=P("ctx", None, "tp"),
        check_vma=False,
    )
```

```python
import functools

import jax
import jax.numpy as jnp
from jax import lax
from jax.experimental import pallas as pl
from jax.experimental.pallas import tpu as pltpu
from jax.sharding import PartitionSpec as P

HD = 128
MESH = pl.DeviceIdType.MESH
NEG = -1e30
CHUNKS = 4
AHEAD = 3
BF = jnp.bfloat16
F32 = jnp.float32


def remote(src, dst, send_sem, recv_sem, device):
    return pltpu.make_async_remote_copy(
        src_ref=src, dst_ref=dst, send_sem=send_sem, recv_sem=recv_sem, device_id=device, device_id_type=MESH
    )


def layer_norm(values, gain):
    centre = jnp.mean(values, axis=-1, keepdims=True)
    centred = values - centre
    variance = jnp.mean(centred * centred, axis=-1, keepdims=True)
    return centred * lax.rsqrt(variance + 1e-05) * gain


def dot(a, b):
    return jnp.dot(a, b, preferred_element_type=F32)


def dot_t(a, b):
    return lax.dot_general(a, b, (((1,), (1,)), ((), ())), preferred_element_type=F32)


class places:
    def __init__(self, tp):
        def other(d):
            return d + 1 - 2 * lax.rem(d, 2)

        self.x = other(tp)
        self.up, self.down, self.far = (lax.rem(tp + step, 8) for step in (2, 6, 4))
        self.up_x, self.down_x, self.far_x = other(self.up), other(self.down), other(self.far)


def layer_kernel(
    lists, tok_ref, gain_attn_ref, wqkv_ref, wout_ref, gain_mlp_ref, wup_ref, wdown_ref, out_ref,
    tok, wqkv, normed, qkv, recv_0, recv_1, colout, ret, acc, maxes, sums,
    att, wo, wu, wd, res, act, terms, share, came,
    tok_sem, load_sem, own_sem, back_sem, send_sem, recv_sem, back_send, back_recv,
    wo_send, wo_recv, wc_send, wc_recv, ag_send, ag_recv, rs_send, rs_recv,
):
    n_ctx, rows, cols = 16, 4, 256
    recv = (recv_0, recv_1)
    part_cols = cols // n_ctx
    ctx = lax.axis_index("ctx")
    tp = lax.axis_index("tp")
    here = places(tp)
    core = lax.rem(ctx, 2)
    sibling = ctx + 1 - 2 * core

    def feats(d):
        return pl.ds(pl.multiple_of(d * 256, 256), 256)

    def row_tokens(r):
        return pl.ds(pl.multiple_of(r * cols, cols), cols)

    def head_lanes(h):
        return pl.ds(pl.multiple_of(tp * 256 + h * HD, HD), HD)

    def tok_load(r):
        return pltpu.make_async_copy(tok_ref.at[row_tokens(r), :], tok.at[row_tokens(r), :], tok_sem.at[r])

    wqkv_load = pltpu.make_async_copy(wqkv_ref, wqkv, load_sem.at[0])
    loads = [
        pltpu.make_async_copy(wout_ref, wo.at[feats(tp), :], load_sem.at[1]),
        pltpu.make_async_copy(wup_ref, wu, load_sem.at[2]),
        pltpu.make_async_copy(wdown_ref, wd, load_sem.at[3]),
    ]
    tok_load(0).start()
    wqkv_load.start()
    for r in range(1, rows):
        tok_load(r).start()

    beside = {"ctx": ctx + 2 - 4 * lax.rem(ctx // 2, 2), "tp": here.x}
    up, down = {"tp": here.up}, {"tp": here.down}

    barrier = pltpu.get_barrier_semaphore()
    for k in range(1, n_ctx):
        pl.semaphore_signal(barrier, inc=1, device_id={"ctx": lax.rem(ctx + k, n_ctx)}, device_id_type=MESH)
    for d in (here.x, here.up, here.down):
        pl.semaphore_signal(barrier, inc=1, device_id={"tp": d}, device_id_type=MESH)
    pl.semaphore_signal(barrier, inc=1, device_id=beside, device_id_type=MESH)

    def norm(r):
        for b in range(cols // 64):
            part = slice(b * 64, (b + 1) * 64)
            tokens = tok[pl.ds(pl.multiple_of(r * cols + b * 64, 64), 64), :]
            normed[lax.rem(r, 2), part, :] = layer_norm(tokens.astype(F32), gain_attn_ref[...]).astype(BF)

    tok_load(0).wait()
    norm(0)
    pl.semaphore_wait(barrier, n_ctx - 1 + 4)

    def w_rows(owner, begin=0, size=64):
        return pl.ds(pl.multiple_of(owner * 256 + core * 128 + begin, 64), size)

    def w_send(kind, owner, piece, device):
        place = wo.at[w_rows(owner, 64 * piece), :]
        source = wout_ref.at[pl.ds(pl.multiple_of(core * 128 + 64 * piece, 64), 64), :] if kind < 6 else place
        return remote(source, place, wo_send.at[kind], wo_recv.at[kind], device)

    w_up = [w_send(0, tp, 0, up), w_send(1, tp, 1, up)]
    w_down = [w_send(2, tp, 1, down), w_send(3, tp, 0, down)]
    w_beside = [w_send(4, tp, 0, beside), w_send(5, tp, 1, beside)]
    w_onward = [w_send(6, here.down, 0, up), w_send(7, here.up, 1, down)]
    w_across = [w_send(8, here.x, 0, down), w_send(9, here.x, 1, up)]
    w_near = [w_send(10, here.down, 0, beside), w_send(11, here.up, 1, beside)]
    w_far = [w_send(12, here.far, 0, beside), w_send(13, here.far, 1, beside)]
    w_all = w_up + w_down + w_beside + w_onward + w_across + w_near + w_far

    def to_sibling(kind, owner, begin=0, size=128):
        place = wo.at[w_rows(owner, begin, size), :]
        return remote(place, place, wc_send.at[kind], wc_recv.at[kind], {"ctx": sibling})

    siblings = [
        to_sibling(kind, owner)
        for kind, owner in enumerate((here.x, here.up, here.down, here.up_x, here.down_x, here.far))
    ] + [to_sibling(6, here.far_x, 0, 64), to_sibling(7, here.far_x, 64, 64)]

    def start_all(copies):
        for copy in copies:
            copy.start()

    def arrive_all(copies):
        for copy in copies:
            copy.wait_recv()

    start_all([w_up[0], w_down[0], w_beside[0], w_up[1], w_down[1], w_beside[1]])

    def col_share(j):
        return pl.ds(pl.multiple_of(j * part_cols, part_cols), part_cols)

    def exchange(h, k):
        source = lax.rem(ctx + n_ctx - k, n_ctx)
        place = recv[h].at[source]
        return remote(place, place, send_sem.at[h, k - 1], recv_sem.at[h, k - 1], {"ctx": source})

    def give_back(h, k):
        j = lax.rem(ctx + k, n_ctx)
        return remote(colout.at[h, j], ret.at[h, ctx], back_send.at[h, k], back_recv.at[h, k], {"ctx": j})

    own_blocks = [
        pltpu.make_async_copy(qkv.at[h, :, col_share(ctx), :], recv[h].at[ctx], own_sem.at[h]) for h in range(2)
    ]
    own_backs = [pltpu.make_async_copy(colout.at[h, ctx], ret.at[h, ctx], back_sem.at[h]) for h in range(2)]

    wqkv_load.wait()
    for r in range(1, rows):
        tok_load(r).wait()

    @pl.loop(0, rows)
    def _(r):
        norm(jnp.minimum(r + 1, rows - 1))
        for n in range(3):
            both = dot(normed[lax.rem(r, 2)], wqkv[n]).astype(BF)
            for h in range(2):
                qkv[h, r, :, n * HD : (n + 1) * HD] = both[:, h * HD : (h + 1) * HD]
        for k in range(1, n_ctx):
            j = lax.rem(ctx + k, n_ctx)
            remote(
                qkv.at[0, r, col_share(j), :], recv[0].at[ctx, r],
                send_sem.at[0, k - 1], recv_sem.at[0, k - 1], {"ctx": j},
            ).start()

    for k in range(1, n_ctx):
        j = lax.rem(ctx + k, n_ctx)
        remote(
            qkv.at[1, :, col_share(j), :], recv[1].at[ctx], send_sem.at[1, k - 1], recv_sem.at[1, k - 1], {"ctx": j}
        ).start()
    for copy in own_blocks + loads:
        copy.start()

    arrive_all([w_up[0], w_down[0]])
    start_all(w_onward + w_near)
    arrive_all([w_beside[0]])
    start_all(w_across[:1])

    causal = lax.broadcasted_iota(jnp.int32, (cols, cols), 1) <= lax.broadcasted_iota(jnp.int32, (cols, cols), 0)

    @pl.loop(0, rows)
    def _(r):
        for h in range(2):
            q, key, val = (qkv[h, r, :, n * HD : (n + 1) * HD] for n in range(3))
            scores = jnp.where(causal, dot_t(q, key) * HD ** (-0.5), NEG)
            top = jnp.max(scores, axis=-1, keepdims=True)
            weights = jnp.exp(scores - top)
            acc[r, :, h * HD : (h + 1) * HD] = dot(weights.astype(BF), val)
            maxes[r, :, h * HD : (h + 1) * HD] = jnp.broadcast_to(top, (cols, HD))
            sums[r, :, h * HD : (h + 1) * HD] = jnp.broadcast_to(jnp.sum(weights, axis=-1, keepdims=True), (cols, HD))

    q_id = lax.broadcasted_iota(jnp.int32, (64, 256), 0)
    k_id = lax.broadcasted_iota(jnp.int32, (64, 256), 1)
    entry = k_id // 64
    same = lax.rem(q_id, 16) == lax.rem(k_id, 16)
    earlier = same & (entry == 0) & (lax.rem(k_id, 64) // 16 < q_id // 16)
    lane = lax.broadcasted_iota(jnp.int32, (64, HD), 1)
    eye = (lax.broadcasted_iota(jnp.int32, (64, HD), 0) == lane).astype(BF)

    def turn(a):
        return lax.dot_general(a, eye[: a.shape[0]], (((0,), (0,)), ((), ())), preferred_element_type=F32)

    def column_block(h, i):
        ids = [lists[l, i] for l in range(4)]
        fresh = []
        for l in range(1, 4):
            new = jnp.int32(1)
            for before in range(l):
                new = new * (ids[l] != ids[before]).astype(jnp.int32)
            fresh.append(new)
        usable = jnp.where(entry == 1, fresh[0], jnp.where(entry == 2, fresh[1], fresh[2]))
        mask = earlier | (same & (entry > 0) & (usable > 0))
        q = recv[h][i, :, :, 0:HD].reshape(64, HD)
        key, val = (
            jnp.concatenate([recv[h][b, :, :, n * HD : (n + 1) * HD].reshape(64, HD) for b in ids], axis=0)
            for n in (1, 2)
        )
        scores = jnp.where(mask, dot_t(q, key) * HD ** (-0.5), NEG)
        top = jnp.max(scores, axis=-1, keepdims=True)
        weights = jnp.where(mask, jnp.exp(scores - top), 0.0)
        total = jnp.sum(weights, axis=-1, keepdims=True)
        colout[h, i, 0:64, :] = (dot(weights.astype(BF), val) / jnp.maximum(total, 1.0)).astype(BF)
        top_hi = top.astype(BF).astype(F32)
        top_mid = (top - top_hi).astype(BF).astype(F32)
        total_hi = total.astype(BF).astype(F32)
        stats = jnp.zeros((64, HD), F32)
        for n, piece in enumerate((top_hi, top_mid, top - top_hi - top_mid, total_hi, total - total_hi)):
            stats = jnp.where(lane == n, piece, stats)
        colout[h, i, 64:80, :] = turn(stats.astype(BF))[0:16, :].astype(BF)

    def column_part(h):
        own_blocks[h].wait()
        for k in range(1, n_ctx):
            exchange(h, k).wait_recv()

        @pl.loop(0, n_ctx // 4)
        def _(group):
            for member in range(4):
                column_block(h, lax.rem(ctx + group * 4 + member, n_ctx))
            for member in range(4):
                k = group * 4 + member

                @pl.when(k == 0)
                def _():
                    own_backs[h].start()

                @pl.when(k > 0)
                def _():
                    give_back(h, k).start()

    def merge(h, j):
        lanes = slice(h * HD, (h + 1) * HD)
        stats = turn(ret[h, j, 64:80, :])[0:64, :]
        col_top = stats[:, 0:1] + stats[:, 1:2] + stats[:, 2:3]
        col_sum = stats[:, 3:4] + stats[:, 4:5]
        row_top, row_sum, row_part = (a[:, col_share(j), lanes].reshape(64, HD) for a in (maxes, sums, acc))
        top = jnp.maximum(row_top, col_top)
        row_scale = jnp.exp(row_top - top)
        col_scale = jnp.exp(col_top - top) * col_sum
        merged = row_part * row_scale + ret[h, j, 0:64, :].astype(F32) * col_scale
        merged = (merged / (row_sum * row_scale + col_scale)).astype(BF)
        for r in range(rows):
            att[pl.ds(pl.multiple_of(r * cols + j * part_cols, part_cols), part_cols), head_lanes(h)] = merged[
                r * part_cols : (r + 1) * part_cols
            ]

    def merge_part(h):
        @pl.loop(0, n_ctx // 4)
        def _(group):
            for member in range(4):
                k = group * 4 + member

                @pl.when(k == 0)
                def _():
                    own_backs[h].wait()

                @pl.when(k > 0)
                def _():
                    give_back(h, k).wait_recv()

            for member in range(4):
                merge(h, lax.rem(ctx + n_ctx - group * 4 - member, n_ctx))

    arrive_all([w_beside[1]])
    start_all(w_across[1:])
    arrive_all([w_up[1], w_down[1]])
    start_all(siblings[:3])
    column_part(0)
    arrive_all(w_onward)
    start_all(w_far)
    start_all(siblings[5:6])
    column_part(1)
    arrive_all(w_across + w_near)
    start_all(siblings[3:5])
    chunks, chunk = CHUNKS, 1024 // CHUNKS
    half = chunk // 2

    def rows_of(c):
        return pl.ds(pl.multiple_of(c * chunk, chunk), chunk)

    def low(c):
        return pl.ds(pl.multiple_of(c * chunk, half), half)

    def high(c):
        return pl.ds(pl.multiple_of(c * chunk + half, half), half)

    def gather(kind, c, rows, owner, device, lanes=None):
        place = att.at[rows, feats(owner) if lanes is None else lanes]
        return remote(place, place, ag_send.at[kind, c], ag_recv.at[kind, c], {"tp": device})

    gathers = (
        lambda c: gather(0, c, rows_of(c), tp, here.x),
        lambda c: gather(1, c, rows_of(c), tp, here.up, head_lanes(0)),
        lambda c: gather(2, c, rows_of(c), tp, here.down, head_lanes(0)),
        lambda c: gather(3, c, rows_of(c), here.x, here.up),
        lambda c: gather(4, c, rows_of(c), here.x, here.down),
        lambda c: gather(5, c, low(c), here.down, here.up),
        lambda c: gather(6, c, high(c), here.up, here.down),
        lambda c: gather(7, c, rows_of(c), here.far, here.x),
        lambda c: gather(8, c, rows_of(c), tp, here.up, head_lanes(1)),
        lambda c: gather(9, c, rows_of(c), tp, here.down, head_lanes(1)),
    )

    def scatter(kind, c, rows, owner, device, slot):
        return remote(
            terms.at[rows, feats(owner)], came.at[slot, rows, :],
            rs_send.at[kind, c], rs_recv.at[kind, c], {"tp": device},
        )

    scatters = (
        lambda c: scatter(0, c, rows_of(c), here.far_x, here.x, 0),
        lambda c: scatter(1, c, rows_of(c), here.up_x, here.up, 1),
        lambda c: scatter(2, c, rows_of(c), here.down_x, here.down, 2),
        lambda c: scatter(3, c, low(c), here.far, here.up, 3),
        lambda c: scatter(4, c, high(c), here.far, here.down, 3),
        lambda c: scatter(5, c, rows_of(c), here.up, here.up, 4),
        lambda c: scatter(6, c, rows_of(c), here.down, here.down, 5),
        lambda c: scatter(7, c, rows_of(c), here.x, here.x, 6),
    )

    def start(copies, kinds, c):
        for kind in kinds:
            copies[kind](c).start()

    def arrive(copies, kinds, c):
        for kind in kinds:
            copies[kind](c).wait_recv()

    def add(rows, owner, slots):
        total = terms[rows, feats(owner)].astype(F32)
        for slot in slots:
            total = total + came[slot, rows, :].astype(F32)
        return total

    def when(c, step):
        @pl.when((c >= 0) & (c < chunks))
        def _():
            step(c)

    def ag_begin(c):
        start(gathers, (8, 9, 0), c)

    def ag_across(c):
        arrive(gathers, (0, 1, 2, 8, 9), c)
        start(gathers, (3, 4, 5, 6), c)

    def ag_far(c):
        arrive(gathers, (5, 6), c)
        start(gathers, (7,), c)

    def ag_end(c):
        arrive(gathers, (3, 4, 7), c)

    def rs_far(c):
        arrive(scatters, (0,), c)
        terms[rows_of(c), feats(here.far)] = add(rows_of(c), here.far, [0]).astype(BF)
        start(scatters, (3, 4), c)

    def rs_across(c):
        arrive(scatters, (1, 2), c)
        terms[rows_of(c), feats(here.x)] = add(rows_of(c), here.x, [1, 2]).astype(BF)
        start(scatters, (7,), c)

    def rs_near(c):
        arrive(scatters, (3,), c)
        terms[low(c), feats(here.up)] = add(low(c), here.up, [3]).astype(BF)
        start(scatters, (5,), c)
        arrive(scatters, (4,), c)
        terms[high(c), feats(here.down)] = add(high(c), here.down, [3]).astype(BF)
        start(scatters, (6,), c)

    def rs_end(c):
        arrive(scatters, (5, 6, 7), c)
        rows = rows_of(c)
        out_ref[rows, :] = (share[rows, :] + add(rows, tp, [4, 5, 6])).astype(BF)

    def compute_up(c):
        rows = rows_of(c)
        for n in range(8):
            cols = slice(n * 256, (n + 1) * 256)
            res[:, cols] = tok[rows, cols].astype(F32) + dot(att[rows, :], wo[:, cols])
        for b in range(chunk // 64):
            part = slice(b * 64, (b + 1) * 64)
            normed[0, part, :] = layer_norm(res[part, :], gain_mlp_ref[...]).astype(BF)
        share[rows, :] = res[:, feats(tp)]
        for n in range(4):
            cols = slice(n * 256, (n + 1) * 256)
            act[:, cols] = jax.nn.gelu(dot(normed[0, 0:chunk, :], wu[:, cols])).astype(BF)

    def compute_down(c):
        rows = rows_of(c)
        order = (here.far_x, here.up_x, here.down_x, here.far, here.x, here.up, here.down, tp)
        for d in order:
            terms[rows, feats(d)] = dot(act[...], wd[:, feats(d)]).astype(BF)
        start(scatters, (0, 1, 2), c)

    merge_part(0)
    for c in range(chunks):
        start(gathers, (1, 2), c)
    merge_part(1)
    for c in range(AHEAD):
        ag_begin(c)
    ag_across(0)
    ag_across(1)
    ag_far(0)
    for copy, onward in zip(w_far, siblings[6:]):
        copy.wait_recv()
        onward.start()
    for copy in loads:
        copy.wait()
    arrive_all(siblings)

    @pl.loop(0, chunks + 3)
    def _(c):
        when(c, ag_end)
        when(c + AHEAD, ag_begin)
        when(c + 2, ag_across)
        when(c + 1, ag_far)
        when(c, compute_up)
        when(c - 1, rs_far)
        when(c, compute_down)
        when(c - 1, rs_across)
        when(c - 2, rs_near)
        when(c - 3, rs_end)

    @pl.loop(0, chunks)
    def _(c):
        for copy in gathers + scatters:
            copy(c).wait_send()

    for copy in w_all + siblings:
        copy.wait_send()
    for h in range(2):
        for k in range(1, n_ctx):
            exchange(h, k).wait_send()
            give_back(h, k).wait_send()


ANY = pl.BlockSpec(memory_space=pl.ANY)
VMEM = pl.BlockSpec(memory_space=pltpu.VMEM)
SMEM = pl.BlockSpec(memory_space=pltpu.SMEM)
DMA = pltpu.SemaphoreType.DMA


def on_device(tokens, block_lists, gain_attn, w_qkv, w_out, gain_mlp, w_up, w_down):
    rows, cols, width = tokens.shape
    flat = tokens.reshape(rows * cols, width)
    out = pl.pallas_call(
        layer_kernel,
        out_shape=jax.ShapeDtypeStruct((rows * cols, 256), BF),
        in_specs=[SMEM, ANY, VMEM, ANY, ANY, VMEM, ANY, ANY],
        out_specs=VMEM,
        scratch_shapes=[
            pltpu.VMEM((1024, 2048), BF),
            pltpu.VMEM((3, 2048, 256), BF),
            pltpu.VMEM((2, 256, 2048), BF),
            pltpu.VMEM((2, 4, 256, 384), BF),
            pltpu.VMEM((16, 4, 16, 384), BF),
            pltpu.VMEM((16, 4, 16, 384), BF),
            pltpu.VMEM((2, 16, 80, 128), BF),
            pltpu.VMEM((2, 16, 80, 128), BF),
            pltpu.VMEM((4, 256, 256), F32),
            pltpu.VMEM((4, 256, 256), F32),
            pltpu.VMEM((4, 256, 256), F32),
            pltpu.VMEM((1024, 2048), BF),
            pltpu.VMEM((2048, 2048), BF),
            pltpu.VMEM((2048, 1024), BF),
            pltpu.VMEM((1024, 2048), BF),
            pltpu.VMEM((1024 // CHUNKS, 2048), F32),
            pltpu.VMEM((1024 // CHUNKS, 1024), BF),
            pltpu.VMEM((1024, 2048), BF),
            pltpu.VMEM((1024, 256), F32),
            pltpu.VMEM((7, 1024, 256), BF),
            DMA((4,)), DMA((4,)), DMA((2,)), DMA((2,)),
            DMA((2, 15)), DMA((2, 15)), DMA((2, 16)), DMA((2, 16)),
            DMA((14,)), DMA((14,)), DMA((8,)), DMA((8,)),
            DMA((10, CHUNKS)), DMA((10, CHUNKS)), DMA((8, CHUNKS)), DMA((8, CHUNKS)),
        ],
        compiler_params=pltpu.CompilerParams(collective_id=0, has_side_effects=True, vmem_limit_bytes=60 << 20),
        name="layer",
    )(
        block_lists.T, flat, gain_attn.reshape(1, width), jnp.transpose(w_qkv, (1, 0, 2)), w_out,
        gain_mlp.reshape(1, width), w_up, w_down,
    )
    return out.reshape(rows, cols, 256)


def solution(mesh):
    return jax.shard_map(
        on_device,
        mesh=mesh,
        in_specs=(
            P("ctx", None, None),
            P(),
            P(),
            P(None, None, "tp"),
            P("tp", None),
            P(),
            P(None, "tp"),
            P("tp", None),
        ),
        out_specs=P("ctx", None, "tp"),
        check_vma=False,
    )
```
